128 devices in a mesh: pipe: 4 (over y_lo, core), expert: 32 (over z, y_hi, x).
Axes of the slice: x: 4, y: 4 (y_hi: 2, y_lo: 2; y = y_hi * 2 + y_lo), z: 4, core: 2. Of those that a mesh axis runs over, the one named last changes fastest.
Arguments:
- tokens_a: bfloat16 [2048, 7168], P('expert', 'pipe'), may hold values from -6 to 6
- routes_a: int32 [2048, 8], P('expert'), may hold values from 0 to 31, all different within a row; in each aligned block of 64 rows (0 to 63, 64 to 127, ...) at most 20 rows name the same one
- gates_a: float32 [2048, 8], P('expert'), may hold values from 0.1 to 1
- tokens_b: bfloat16 [2048, 7168], P('expert', 'pipe'), may hold values from -6 to 6
- routes_b: int32 [2048, 8], P('expert'), may hold values from 0 to 31, all different within a row; in each aligned block of 64 rows (0 to 63, 64 to 127, ...) at most 20 rows name the same one
- gates_b: float32 [2048, 8], P('expert'), may hold values from 0.1 to 1
- grad_b: bfloat16 [2048, 7168], P('expert', 'pipe'), may hold values from -6 to 6
- w_gate: bfloat16 [32, 7168, 1024], P('expert', 'pipe'), may hold values from -0.0625 to 0.0625
- w_up: bfloat16 [32, 7168, 1024], P('expert', 'pipe'), may hold values from -0.0625 to 0.0625
- w_down: bfloat16 [32, 1024, 7168], P('expert', None, 'pipe'), may hold values from -0.1875 to 0.1875
Outputs:
- mixed_a: bfloat16 [2048, 7168], P('expert', 'pipe')
- grad_tokens_b: bfloat16 [2048, 7168], P('expert', 'pipe')
- grad_w_gate: bfloat16 [32, 7168, 1024], P('expert', 'pipe')
- grad_w_up: bfloat16 [32, 7168, 1024], P('expert', 'pipe')
- grad_w_down: bfloat16 [32, 1024, 7168], P('expert', None, 'pipe')
The draws below stay inside these ranges and needn't reach their ends.
Inputs may be any that keep to these rules, and one draw needn't show every extreme that they name: `routes_a`: within the rows of one device (aligned blocks of 64 rows) no expert is named more than 20 times, a bound that some block reaches; the 8 experts of a row differ. `routes_b`: as for routes_a.
All inputs are finite; a program needn't handle non-finite values.
Results may differ from the reference program's by a relative error of at most 0.024.
Values may be sent and summed in bfloat16 or wider, within the bound.
No kernel may reach another device: no remote copies, remote signals or barrier semaphores. Data moves between devices by JAX's collectives and lax.ppermute only.
A program may use at most 128 MiB of HBM per device.

```python
import math
import jax
import jax.numpy as jnp
import numpy as np
from jax import lax

D = 7168
HID = 1024
TOP = 8
TOK_DEV = 64
EXPERTS = 32
CAP = 20
TOKENS = 2048
N_PIPE = 4
N_EXPERT = 32


def block_levels(own_key, extent, cuts, low, high):
    loudness = 1.0
    for dim, shards_of in cuts:
        draws = jax.random.uniform(jax.random.fold_in(jax.random.fold_in(own_key, 6), dim), (shards_of,), jnp.float32, low / len(cuts), high / len(cuts))
        loudness = loudness * jnp.repeat(jnp.exp(draws), extent[dim] // shards_of).reshape((-1,) + (1,) * (len(extent) - 1 - dim))
    return loudness


def deal_out(key, own, number, rows, count, top, limit, slope):
    sequence = jax.random.permutation(key, count)
    packed, ordinary = portions_of(count, rows * top, limit, slope, True), portions_of(count, rows * top, limit, slope, False)
    places = jnp.arange(count)

    def named(lengths, offset_by):
        used = int((lengths > 0).sum())
        fixed = max(1, used // 4)
        passed = fixed + (places - fixed + offset_by * (used - fixed)) % max(1, count - fixed)
        return jnp.zeros((count,), jnp.int32).at[sequence[jnp.where(places < fixed, places, passed)]].set(jnp.asarray(lengths, jnp.int32))

    lengths = jnp.where(number % 4 == 0, named(packed, number // 4), named(ordinary, number - number // 4 - 1))
    mixed = jax.random.permutation(jax.random.fold_in(own, 3), count)
    giver, taker = mixed[0:count // 2 * 2:2], mixed[1:count // 2 * 2:2]
    slack = jnp.minimum(lengths[giver] - 1, limit - lengths[taker]) // 2
    slack = jnp.where((giver == sequence[0]) | (taker == sequence[0]) | (lengths[taker] == 0), 0, jnp.maximum(slack, 0))
    passed = jax.random.randint(jax.random.fold_in(own, 4), (count // 2,), 0, 1 << 20) % (slack + 1)
    lengths = lengths.at[giver].add(-passed).at[taker].add(passed)
    labels = jnp.searchsorted(jnp.cumsum(lengths), jnp.arange(rows * top), side="right").astype(jnp.int32)
    table = labels.reshape(top, rows).T
    table = table[jax.random.permutation(jax.random.fold_in(own, 1), rows)]
    offset_by = jax.random.randint(jax.random.fold_in(own, 2), (rows, 1), 0, top)
    return jnp.take_along_axis(table, (jnp.arange(top)[None, :] + offset_by) % top, axis=1)


def portions_of(number_of, total, most, skew, full):
    loads = [(1 << 20) // math.isqrt(standing ** skew) + 1 for standing in range(1, number_of + 1)]
    largest = most if full else min(most, max(-(-total // number_of), total * loads[0] // sum(loads)))
    least = 1 if total - largest >= number_of - 1 else 0
    counts, rest = [largest] + [least] * (number_of - 1), total - largest - least * (number_of - 1)
    while rest > 0:
        free = [i for i in range(1, number_of) if counts[i] < largest] or [i for i in range(1, number_of) if counts[i] < most]
        pool, left = sum([loads[i] for i in free]), rest
        for i in free:
            extra = min(most - counts[i], max(1, left * loads[i] // pool), rest)
            counts[i] = counts[i] + extra
            rest = rest - extra
    return np.array(counts)


def bell_draw(rng, extent, scale, most, shards=(), kind=jnp.bfloat16):
    result = scale * jax.random.normal(rng, extent, jnp.float32)
    if shards:
        result = result * block_levels(rng, extent, shards, -0.22, 0.18)
    return jnp.clip(result, -most, most).astype(kind)


def setup_inputs(seed: int = 0) -> dict:
    arg_keys = jax.random.split(jax.random.key(seed), 11)
    tokens_a = bell_draw(arg_keys[0], (TOKENS, D), 1.0, 6.0, ((0, 32), (1, 4)))
    routes_a_keys = jax.random.split(jax.random.fold_in(arg_keys[1], 1), TOKENS // TOK_DEV)
    routes_a_turns = jax.random.permutation(jax.random.fold_in(arg_keys[1], 3), TOKENS // TOK_DEV)
    routes_a = jax.vmap(lambda own, number: deal_out(jax.random.fold_in(arg_keys[1], 2), own, number, TOK_DEV, EXPERTS, TOP, CAP, 2))(routes_a_keys, routes_a_turns).reshape((TOKENS, TOP))
    gates_a = jnp.clip(0.1 + 0.9 * jax.random.uniform(arg_keys[2], (TOKENS, TOP), jnp.float32) ** block_levels(arg_keys[2], (TOKENS, TOP), ((0, 32),), -0.2, 0.2), 0.1, 1.0)
    tokens_b = bell_draw(arg_keys[3], (TOKENS, D), 1.0, 6.0, ((0, 32), (1, 4)))
    routes_b_keys = jax.random.split(jax.random.fold_in(arg_keys[4], 1), TOKENS // TOK_DEV)
    routes_b_turns = jax.random.permutation(jax.random.fold_in(arg_keys[4], 3), TOKENS // TOK_DEV)
    routes_b = jax.vmap(lambda own, number: deal_out(jax.random.fold_in(arg_keys[4], 2), own, number, TOK_DEV, EXPERTS, TOP, CAP, 2))(routes_b_keys, routes_b_turns).reshape((TOKENS, TOP))
    gates_b = jnp.clip(0.1 + 0.9 * jax.random.uniform(arg_keys[5], (TOKENS, TOP), jnp.float32) ** block_levels(arg_keys[5], (TOKENS, TOP), ((0, 32),), -0.2, 0.2), 0.1, 1.0)
    grad_b = bell_draw(arg_keys[6], (TOKENS, D), 1.0, 6.0, ((0, 32), (1, 4)))
    w_gate = bell_draw(arg_keys[7], (EXPERTS, D, HID), D ** -0.5, 0.0625, ((0, 32), (1, 4)))
    w_up = bell_draw(arg_keys[8], (EXPERTS, D, HID), D ** -0.5, 0.0625, ((0, 32), (1, 4)))
    w_down = bell_draw(arg_keys[9], (EXPERTS, HID, D), HID ** -0.5, 0.1875, ((0, 32), (2, 4)))
    return {"tokens_a": tokens_a, "routes_a": routes_a, "gates_a": gates_a, "tokens_b": tokens_b, "routes_b": routes_b, "gates_b": gates_b, "grad_b": grad_b, "w_gate": w_gate, "w_up": w_up, "w_down": w_down}


def silu_slope(values):
    sigma = jax.nn.sigmoid(values)
    return sigma * (1.0 + values * (1.0 - sigma))


def slot_table(routes):
    blocks = routes.reshape(N_EXPERT, TOK_DEV * TOP)
    onehot = (blocks[:, :, None] == jnp.arange(EXPERTS, dtype=jnp.int32)[None, None, :]).astype(jnp.int32)
    position = jnp.sum(onehot * (jnp.cumsum(onehot, axis=1) - 1), axis=2)
    source = jnp.arange(N_EXPERT, dtype=jnp.int32)[:, None]
    return (blocks * (N_EXPERT * CAP) + source * CAP + position).reshape(-1).astype(jnp.int32)


def pack_slots(values, index):
    buffer = jnp.zeros((EXPERTS * N_EXPERT * CAP, D), values.dtype).at[index].set(values)
    return buffer.reshape(EXPERTS, N_EXPERT * CAP, D)


def split_sum(product):
    return lax.optimization_barrier(product.astype(jnp.bfloat16)).astype(jnp.float32).sum(axis=0)


def expert_pass(items):
    inputs_a, inputs_b, scaled_b, weight_gate, weight_up, weight_down = items
    quarter = D // N_PIPE
    gate_blocks = weight_gate.reshape(N_PIPE, quarter, HID).astype(jnp.float32)
    up_blocks = weight_up.reshape(N_PIPE, quarter, HID).astype(jnp.float32)

    def hidden_layer(inputs):
        pieces = inputs.reshape(-1, N_PIPE, quarter).astype(jnp.float32)
        gate_sum = split_sum(jnp.einsum("sqd,qdh->qsh", pieces, gate_blocks))
        up_sum = split_sum(jnp.einsum("sqd,qdh->qsh", pieces, up_blocks))
        return (jax.nn.silu(gate_sum) * up_sum).astype(jnp.bfloat16), gate_sum, up_sum

    hidden_a, _, _ = hidden_layer(inputs_a)
    out_a = jnp.dot(hidden_a, weight_down, preferred_element_type=jnp.float32).astype(jnp.bfloat16)
    hidden_b, gate_b, up_b = hidden_layer(inputs_b)
    grad_pieces = scaled_b.reshape(-1, N_PIPE, quarter).astype(jnp.float32)
    down_blocks = weight_down.reshape(HID, N_PIPE, quarter).astype(jnp.float32)
    grad_hidden = split_sum(jnp.einsum("sqd,hqd->qsh", grad_pieces, down_blocks))
    d_gate = (grad_hidden * up_b * silu_slope(gate_b)).astype(jnp.bfloat16)
    d_up = (grad_hidden * jax.nn.silu(gate_b)).astype(jnp.bfloat16)
    grad_inputs = (jnp.dot(d_gate, weight_gate.T, preferred_element_type=jnp.float32)
                   + jnp.dot(d_up, weight_up.T, preferred_element_type=jnp.float32)).astype(jnp.bfloat16)
    grad_gate = jnp.dot(inputs_b.T, d_gate, preferred_element_type=jnp.float32).astype(jnp.bfloat16)
    grad_up = jnp.dot(inputs_b.T, d_up, preferred_element_type=jnp.float32).astype(jnp.bfloat16)
    grad_down = jnp.dot(hidden_b.T, scaled_b, preferred_element_type=jnp.float32).astype(jnp.bfloat16)
    return out_a, grad_inputs, grad_gate, grad_up, grad_down


def reference(tokens_a, routes_a, gates_a, tokens_b, routes_b, gates_b, grad_b, w_gate, w_up, w_down):
    index_a = slot_table(routes_a)
    index_b = slot_table(routes_b)
    slots_a = pack_slots(jnp.repeat(tokens_a, TOP, axis=0), index_a)
    slots_b = pack_slots(jnp.repeat(tokens_b, TOP, axis=0), index_b)
    scaled = (gates_b[:, :, None] * grad_b[:, None, :].astype(jnp.float32)).astype(jnp.bfloat16)
    scaled_slots = pack_slots(scaled.reshape(-1, D), index_b)
    out_a, grad_inputs, grad_gate, grad_up, grad_down = lax.map(
        expert_pass, (slots_a, slots_b, scaled_slots, w_gate, w_up, w_down))
    picked_a = out_a.reshape(-1, D)[index_a].astype(jnp.float32).reshape(TOKENS, TOP, D)
    mixed_a = jnp.sum(picked_a * gates_a[:, :, None], axis=1).astype(jnp.bfloat16)
    picked_b = grad_inputs.reshape(-1, D)[index_b].astype(jnp.float32).reshape(TOKENS, TOP, D)
    grad_tokens_b = jnp.sum(picked_b, axis=1).astype(jnp.bfloat16)
    return mixed_a, grad_tokens_b, grad_gate, grad_up, grad_down
```

```python
import jax
import jax.numpy as jnp
from jax import lax
from jax.sharding import PartitionSpec as P

BOTH = ("pipe", "expert")
PIPE = 4
GROUPS = 32
bf16 = jnp.bfloat16
f32 = jnp.float32


def split_place(pipe, expert):
    return pipe // 2, pipe % 2, expert // 8, (expert // 4) % 2, expert % 4


def moved(move):
    pairs = []
    for pipe in range(PIPE):
        for expert in range(GROUPS):
            yl, c, z, yh, x = move(*split_place(pipe, expert))
            target = (yl * 2 + c) * GROUPS + z * 8 + yh * 4 + x
            pairs.append((pipe * GROUPS + expert, target))
    return pairs


def send(value, move):
    return lax.ppermute(value, BOTH, moved(move))


def shift_near(d):
    def move(yl, c, z, yh, x):
        return (yl, c, (z + d) % 4, yh, x) if c == 0 else (yl, c, z, yh, (x + d) % 4)

    return move


def shift_far(d):
    def move(yl, c, z, yh, x):
        return (yl, c, z, yh, (x + d) % 4) if c == 0 else (yl, c, (z + d) % 4, yh, x)

    return move


def flip_row(yl, c, z, yh, x):
    return (yl, c, z, 1 - yh, x)


def flip_core(yl, c, z, yh, x):
    return (yl, 1 - c, z, yh, x)


def flip_chip(yl, c, z, yh, x):
    return (1 - yl, c, z, yh, x)


def dot(a, b):
    return jnp.dot(a, b, preferred_element_type=f32)


def dot_t(a, b):
    return lax.dot_general(a, b, (((1,), (1,)), ((), ())), preferred_element_type=f32)


def t_dot(a, b):
    return lax.dot_general(a, b, (((0,), (0,)), ((), ())), preferred_element_type=f32)


def silu_slope(values):
    sigma = jax.nn.sigmoid(values)
    return sigma * (1.0 + values * (1.0 - sigma))


def two_parts(values):
    high = lax.reduce_precision(values, 8, 7)
    return high.astype(bf16), (values - high).astype(bf16)


def spread(rows):
    other = send(rows, flip_row)
    pair = jnp.concatenate([rows, other], axis=0)
    far = send(pair, shift_near(2))
    up = send(pair, shift_near(1))
    down = send(pair, shift_near(3))
    return jnp.concatenate([pair, up, far, down], axis=0)


def exchange(chunks, back=False):
    sign = -1 if back else 1
    two = send(chunks[2], shift_far(2))
    one = send(chunks[1], shift_far(sign % 4))
    three = send(chunks[3], shift_far(-sign % 4))
    return jnp.concatenate([chunks[0], one, two, three], axis=0)


def gather_back(partial, rows):
    pair = 2 * rows
    sent = partial.astype(bf16)
    two = send(sent[2 * pair : 3 * pair], shift_near(2))
    one = send(sent[pair : 2 * pair], shift_near(3))
    three = send(sent[3 * pair :], shift_near(1))
    total = partial[:pair] + one.astype(f32) + two.astype(f32) + three.astype(f32)
    other = send(total[rows:].astype(bf16), flip_row)
    return (total[:rows] + other.astype(f32)).astype(bf16)


def across(value, blocks=4):
    rows, cols = value.shape
    piece = rows // (blocks * blocks)
    cut = value.reshape(blocks, blocks, piece, cols)
    return jnp.swapaxes(cut, 0, 1).reshape(rows, cols)


def per_device(
    tokens_a, routes_a, gates_a, tokens_b, routes_b, gates_b, grad_b, w_gate, w_up, w_down
):
    rows, quarter = tokens_a.shape
    top_k = routes_a.shape[1]
    experts = GROUPS
    capacity = min(rows, 5 * rows * top_k // (4 * experts))
    half = w_gate.shape[2] // 2
    w_gate, w_up, w_down = w_gate[0], w_up[0], w_down[0]
    core = lax.axis_index("pipe") % 2
    mine = lax.axis_index("expert")
    step = jnp.arange(4, dtype=jnp.int32)
    along_x = mine - mine % 4 + (mine + step) % 4
    along_z = (mine + 8 * step) % 32
    wanted = jnp.where(core == 0, along_x, along_z).astype(f32)

    high_a, low_a = two_parts(gates_a)
    high_b, low_b = two_parts(gates_b)
    info = jnp.concatenate(
        [routes_a.astype(bf16), high_a, low_a, routes_b.astype(bf16), high_b, low_b], axis=1
    )
    info = jnp.pad(info, ((0, 0), (0, 128 - info.shape[1])))
    all_a = spread(jnp.concatenate([tokens_a, info], axis=1))
    all_info = all_a[:, quarter:].astype(f32).T
    all_a = all_a[:, :quarter]
    all_b = spread(jnp.concatenate([tokens_b, grad_b], axis=1))

    count = 8 * rows
    token = jnp.arange(count, dtype=jnp.int32)
    block = token // rows
    earlier = (
        (token[:, None] < token[None, :]) & (block[:, None] == block[None, :])
    ).astype(bf16)
    size = 8 * capacity

    def picks(base):
        routes = all_info[base : base + top_k]
        gates = all_info[base + top_k : base + 2 * top_k] + all_info[base + 2 * top_k : base + 3 * top_k]
        same = routes[None, :, :] == wanted[:, None, None]
        hit = jnp.any(same, axis=1)
        gate = jnp.sum(jnp.where(same, gates[None], 0.0), axis=1)
        position = dot(hit.astype(bf16), earlier).astype(jnp.int32)
        slot = jnp.where(hit, block[None, :] * capacity + position, -1)
        chosen = slot[:, None, :] == jnp.arange(size, dtype=jnp.int32)[None, :, None]
        weighted = jnp.where(chosen, gate[:, None, :], 0.0)
        return chosen.reshape(4 * size, count), weighted.reshape(4 * size, count)

    chosen_a, weighted_a = picks(0)
    chosen_b, weighted_b = picks(3 * top_k)
    chosen_a = chosen_a.astype(bf16)
    chosen_b = chosen_b.astype(bf16)
    slot_gate_b = jnp.sum(weighted_b, axis=1, keepdims=True)

    def chunks(value):
        return [value[d * size : (d + 1) * size] for d in range(4)]

    xa = exchange(chunks(dot(chosen_a, all_a).astype(bf16)))
    packed_b = dot(chosen_b, all_b[:, :quarter]).astype(bf16)
    packed_g = (dot(chosen_b, all_b[:, quarter:]) * slot_gate_b).astype(bf16)
    both_b = exchange(chunks(jnp.concatenate([packed_b, packed_g], axis=1)))
    xb = both_b[:, :quarter]
    gb = both_b[:, quarter:]

    def shares(parts):
        kept, given = [], []
        for part in parts:
            low, top = part[:, :half], part[:, half:]
            kept.append(jnp.where(core == 0, low, top))
            given.append(jnp.where(core == 0, top, low).astype(bf16))
        got = send(jnp.concatenate(given, axis=1), flip_core)
        got = across(got)
        own = jnp.concatenate(kept, axis=1) + got.astype(f32)
        far = send(own.astype(bf16), flip_chip)
        total = own + far.astype(f32)
        return [total[:, i * half : (i + 1) * half] for i in range(len(parts))]

    def whole(halves):
        own = jnp.concatenate(halves, axis=1)
        got = across(send(own, flip_core))
        out = []
        for i in range(len(halves)):
            a, b = own[:, i * half : (i + 1) * half], got[:, i * half : (i + 1) * half]
            out.append(
                jnp.concatenate([jnp.where(core == 0, a, b), jnp.where(core == 0, b, a)], axis=1)
            )
        return out

    def combine(weights, value):
        back = exchange(chunks(value), back=True)
        return gather_back(t_dot(weights, back), rows)

    gate_a, up_a = shares([dot(xa, w_gate), dot(xa, w_up)])
    (hidden_a,) = whole([(jax.nn.silu(gate_a) * up_a).astype(bf16)])
    out_a = dot(hidden_a, w_down).astype(bf16)
    mixed_a = combine(weighted_a.astype(bf16), out_a)

    gate_b, up_b, dh = shares([dot(xb, w_gate), dot(xb, w_up), dot_t(gb, w_down)])
    act = jax.nn.silu(gate_b)
    hidden_b, d_gate, d_up = whole(
        [
            (act * up_b).astype(bf16),
            (dh * up_b * silu_slope(gate_b)).astype(bf16),
            (dh * act).astype(bf16),
        ]
    )
    dxb = (dot_t(d_gate, w_gate) + dot_t(d_up, w_up)).astype(bf16)
    grad_tokens_b = combine(chosen_b, dxb)
    grad_gate = t_dot(xb, d_gate).astype(bf16)
    grad_up = t_dot(xb, d_up).astype(bf16)
    grad_down = t_dot(hidden_b, gb).astype(bf16)
    return (mixed_a, grad_tokens_b, grad_gate[None], grad_up[None], grad_down[None])


def solution(mesh):
    return jax.shard_map(
        per_device,
        mesh=mesh,
        in_specs=(
            P("expert", "pipe"),
            P("expert", None),
            P("expert", None),
            P("expert", "pipe"),
            P("expert", None),
            P("expert", None),
            P("expert", "pipe"),
            P("expert", "pipe", None),
            P("expert", "pipe", None),
            P("expert", None, "pipe"),
        ),
        out_specs=(
            P("expert", "pipe"),
            P("expert", "pipe"),
            P("expert", "pipe", None),
            P("expert", "pipe", None),
            P("expert", None, "pipe"),
        ),
        check_vma=False,
    )
```

```python
import jax
import jax.numpy as jnp
from jax import lax
from jax.sharding import PartitionSpec as P

BOTH = ("pipe", "expert")
PIPE = 4
GROUPS = 32
bf16 = jnp.bfloat16
f32 = jnp.float32


def after(value, *others):
    return lax.optimization_barrier((value, others))[0]


def split_place(pipe, expert):
    return pipe // 2, pipe % 2, expert // 8, (expert // 4) % 2, expert % 4


def moved(move):
    pairs = []
    for pipe in range(PIPE):
        for expert in range(GROUPS):
            yl, c, z, yh, x = move(*split_place(pipe, expert))
            target = (yl * 2 + c) * GROUPS + z * 8 + yh * 4 + x
            pairs.append((pipe * GROUPS + expert, target))
    return pairs


def send(value, move):
    return lax.ppermute(value, BOTH, moved(move))


def shift_near(d):
    def move(yl, c, z, yh, x):
        return (yl, c, (z + d) % 4, yh, x) if c == 0 else (yl, c, z, yh, (x + d) % 4)

    return move


def shift_far(d):
    def move(yl, c, z, yh, x):
        return (yl, c, z, yh, (x + d) % 4) if c == 0 else (yl, c, (z + d) % 4, yh, x)

    return move


def flip_row(yl, c, z, yh, x):
    return (yl, c, z, 1 - yh, x)


def flip_core(yl, c, z, yh, x):
    return (yl, 1 - c, z, yh, x)


def flip_chip(yl, c, z, yh, x):
    return (1 - yl, c, z, yh, x)


def dot(a, b):
    return jnp.dot(a, b, preferred_element_type=f32)


def dot_t(a, b):
    return lax.dot_general(a, b, (((1,), (1,)), ((), ())), preferred_element_type=f32)


def t_dot(a, b):
    return lax.dot_general(a, b, (((0,), (0,)), ((), ())), preferred_element_type=f32)


def silu_slope(values):
    sigma = jax.nn.sigmoid(values)
    return sigma * (1.0 + values * (1.0 - sigma))


def two_parts(values):
    high = lax.reduce_precision(values, 8, 7)
    return high.astype(bf16), (values - high).astype(bf16)


def spread(rows):
    other = send(rows, flip_row)
    pair = jnp.concatenate([rows, other], axis=0)
    far = send(pair, shift_near(2))
    up = send(pair, shift_near(1))
    down = send(pair, shift_near(3))
    return jnp.concatenate([pair, up, far, down], axis=0)


def exchange(chunks, back=False):
    sign = -1 if back else 1
    two = send(chunks[2], shift_far(2))
    one = send(chunks[1], shift_far(sign % 4))
    three = send(chunks[3], shift_far(-sign % 4))
    return jnp.concatenate([chunks[0], one, two, three], axis=0)


def gather_back(partial, rows, *others):
    pair = 2 * rows
    sent = partial.astype(bf16)
    two = send(sent[2 * pair : 3 * pair], shift_near(2))
    one = send(sent[pair : 2 * pair], shift_near(3))
    three = send(sent[3 * pair :], shift_near(1))
    one, two, three = after((one, two, three), *others)
    total = partial[:pair] + one.astype(f32) + two.astype(f32) + three.astype(f32)
    other = send(total[rows:].astype(bf16), flip_row)
    return (total[:rows] + other.astype(f32)).astype(bf16)


def across(value, blocks=4):
    rows, cols = value.shape
    piece = rows // (blocks * blocks)
    cut = value.reshape(blocks, blocks, piece, cols)
    return jnp.swapaxes(cut, 0, 1).reshape(rows, cols)


def per_device(
    tokens_a, routes_a, gates_a, tokens_b, routes_b, gates_b, grad_b, w_gate, w_up, w_down
):
    rows, quarter = tokens_a.shape
    top_k = routes_a.shape[1]
    experts = GROUPS
    capacity = min(rows, 5 * rows * top_k // (4 * experts))
    half = w_gate.shape[2] // 2
    w_gate, w_up, w_down = w_gate[0], w_up[0], w_down[0]
    core = lax.axis_index("pipe") % 2
    mine = lax.axis_index("expert")
    step = jnp.arange(4, dtype=jnp.int32)
    along_x = mine - mine % 4 + (mine + step) % 4
    along_z = (mine + 8 * step) % 32
    wanted = jnp.where(core == 0, along_x, along_z).astype(f32)

    high_a, low_a = two_parts(gates_a)
    high_b, low_b = two_parts(gates_b)
    info = sum(
        jnp.pad(part.astype(f32), ((0, 0), (i * top_k, 128 - (i + 1) * top_k)))
        for i, part in enumerate([routes_a, high_a, low_a, routes_b, high_b, low_b])
    ).astype(bf16)
    all_a = spread(jnp.concatenate([tokens_a, info], axis=1))
    all_info = all_a[:, quarter:].astype(f32).T
    all_a = all_a[:, :quarter]
    all_b = spread(jnp.concatenate([tokens_b, grad_b], axis=1))

    count = 8 * rows
    token = jnp.arange(count, dtype=jnp.int32)
    block = token // rows
    earlier = (
        (token[:, None] < token[None, :]) & (block[:, None] == block[None, :])
    ).astype(bf16)
    size = 8 * capacity

    def picks(base):
        routes = all_info[base : base + top_k]
        gates = all_info[base + top_k : base + 2 * top_k] + all_info[base + 2 * top_k : base + 3 * top_k]
        same = routes[None, :, :] == wanted[:, None, None]
        hit = jnp.any(same, axis=1)
        gate = jnp.sum(jnp.where(same, gates[None], 0.0), axis=1)
        position = dot(hit.astype(bf16), earlier).astype(jnp.int32)
        slot = jnp.where(hit, block[None, :] * capacity + position, -1)
        chosen = slot[:, None, :] == jnp.arange(size, dtype=jnp.int32)[None, :, None]
        weighted = jnp.where(chosen, gate[:, None, :], 0.0)
        return chosen.reshape(4 * size, count), weighted.reshape(4 * size, count)

    chosen_a, weighted_a = picks(0)
    chosen_b, weighted_b = picks(3 * top_k)
    chosen_a = chosen_a.astype(bf16)
    chosen_b = chosen_b.astype(bf16)
    slot_gate_b = jnp.sum(weighted_b, axis=1, keepdims=True)

    def chunks(value):
        return [value[d * size : (d + 1) * size] for d in range(4)]

    def given(parts):
        kept, gone = [], []
        for part in parts:
            low, top = part[:, :half], part[:, half:]
            kept.append(jnp.where(core == 0, low, top))
            gone.append(jnp.where(core == 0, top, low).astype(bf16))
        got = across(send(jnp.concatenate(gone, axis=1), flip_core))
        own = jnp.concatenate(kept, axis=1) + got.astype(f32)
        return own, own.astype(bf16)

    def halves(own, far):
        total = own + far.astype(f32)
        return [total[:, i : i + half] for i in range(0, total.shape[1], half)]

    def whole(parts):
        own = jnp.concatenate(parts, axis=1)
        got = across(send(own, flip_core))
        out = []
        for i in range(len(parts)):
            a, b = own[:, i * half : (i + 1) * half], got[:, i * half : (i + 1) * half]
            out.append(
                jnp.concatenate([jnp.where(core == 0, a, b), jnp.where(core == 0, b, a)], axis=1)
            )
        return out

    pack_a = dot(chosen_a, all_a).astype(bf16)
    recv_a = exchange(chunks(pack_a))
    pack_b = jnp.concatenate(
        [
            dot(chosen_b, all_b[:, :quarter]).astype(bf16),
            (dot(chosen_b, all_b[:, quarter:]) * slot_gate_b).astype(bf16),
        ],
        axis=1,
    )
    recv_b = exchange(chunks(pack_b))

    xa = after(recv_a, pack_b)
    own_a, sent_a = given([dot(xa, w_gate), dot(xa, w_up)])
    far_a = send(sent_a, flip_chip)

    both_b = after(recv_b, sent_a)
    xb, gb = both_b[:, :quarter], both_b[:, quarter:]
    own_b, sent_b = given([dot(xb, w_gate), dot(xb, w_up), dot_t(gb, w_down)])
    far_b = send(sent_b, flip_chip)

    gate_a, up_a = halves(own_a, after(far_a, sent_b))
    (hidden_a,) = whole([(jax.nn.silu(gate_a) * up_a).astype(bf16)])
    out_a = dot(hidden_a, w_down).astype(bf16)
    partial_a = t_dot(weighted_a.astype(bf16), exchange(chunks(out_a), back=True))

    gate_b, up_b, dh = halves(own_b, after(far_b, partial_a))
    act = jax.nn.silu(gate_b)
    hidden_b, d_gate, d_up = whole(
        [
            (act * up_b).astype(bf16),
            (dh * up_b * silu_slope(gate_b)).astype(bf16),
            (dh * act).astype(bf16),
        ]
    )
    dxb = (dot_t(d_gate, w_gate) + dot_t(d_up, w_up)).astype(bf16)
    mixed_a = gather_back(partial_a, rows, dxb)
    partial_b = t_dot(chosen_b, exchange(chunks(dxb), back=True))
    grad_tokens_b = gather_back(partial_b, rows)
    grad_gate = t_dot(xb, d_gate).astype(bf16)
    grad_up = t_dot(xb, d_up).astype(bf16)
    grad_down = t_dot(hidden_b, gb).astype(bf16)
    return (mixed_a, grad_tokens_b, grad_gate[None], grad_up[None], grad_down[None])


def solution(mesh):
    return jax.shard_map(
        per_device,
        mesh=mesh,
        in_specs=(
            P("expert", "pipe"),
            P("expert", None),
            P("expert", None),
            P("expert", "pipe"),
            P("expert", None),
            P("expert", None),
            P("expert", "pipe"),
            P("expert", "pipe", None),
            P("expert", "pipe", None),
            P("expert", None, "pipe"),
        ),
        out_specs=(
            P("expert", "pipe"),
            P("expert", "pipe"),
            P("expert", "pipe", None),
            P("expert", "pipe", None),
            P("expert", None, "pipe"),
        ),
        check_vma=False,
    )
```

```python
import jax
import jax.numpy as jnp
from jax import lax
from jax.sharding import PartitionSpec as P

BOTH = ("pipe", "expert")
PIPE = 4
GROUPS = 32
bf16 = jnp.bfloat16
f32 = jnp.float32


def after(value, *others):
    return lax.optimization_barrier((value, others))[0]


def split_place(pipe, expert):
    return pipe // 2, pipe % 2, expert // 8, (expert // 4) % 2, expert % 4


def moved(move):
    pairs = []
    for pipe in range(PIPE):
        for expert in range(GROUPS):
            yl, c, z, yh, x = move(*split_place(pipe, expert))
            target = (yl * 2 + c) * GROUPS + z * 8 + yh * 4 + x
            pairs.append((pipe * GROUPS + expert, target))
    return pairs


def send(value, move):
    return lax.ppermute(value, BOTH, moved(move))


def shift_near(d):
    def move(yl, c, z, yh, x):
        return (yl, c, (z + d) % 4, yh, x) if c == 0 else (yl, c, z, yh, (x + d) % 4)

    return move


def shift_far(d):
    def move(yl, c, z, yh, x):
        return (yl, c, z, yh, (x + d) % 4) if c == 0 else (yl, c, (z + d) % 4, yh, x)

    return move


def flip_row(yl, c, z, yh, x):
    return (yl, c, z, 1 - yh, x)


def flip_core(yl, c, z, yh, x):
    return (yl, 1 - c, z, yh, x)


def flip_chip(yl, c, z, yh, x):
    return (1 - yl, c, z, yh, x)


def dot(a, b):
    return jnp.dot(a, b, preferred_element_type=f32)


def dot_t(a, b):
    return lax.dot_general(a, b, (((1,), (1,)), ((), ())), preferred_element_type=f32)


def t_dot(a, b):
    return lax.dot_general(a, b, (((0,), (0,)), ((), ())), preferred_element_type=f32)


def silu_slope(values):
    sigma = jax.nn.sigmoid(values)
    return sigma * (1.0 + values * (1.0 - sigma))


def two_parts(values):
    high = lax.reduce_precision(values, 8, 7)
    return high.astype(bf16), (values - high).astype(bf16)


def spread(rows):
    other = send(rows, flip_row)
    pair = jnp.concatenate([rows, other], axis=0)
    far = send(pair, shift_near(2))
    up = send(pair, shift_near(1))
    down = send(pair, shift_near(3))
    return pair, up, far, down


def exchange(chunks, back=False):
    sign = -1 if back else 1
    two = send(chunks[2], shift_far(2))
    one = send(chunks[1], shift_far(sign % 4))
    three = send(chunks[3], shift_far(-sign % 4))
    return jnp.concatenate([chunks[0], one, two, three], axis=0)


def gather_back(partial, rows, *others):
    pair = 2 * rows
    sent = partial.astype(bf16)
    two = send(sent[2 * pair : 3 * pair], shift_near(2))
    one = send(sent[pair : 2 * pair], shift_near(3))
    three = send(sent[3 * pair :], shift_near(1))
    one, two, three = after((one, two, three), *others)
    total = partial[:pair] + one.astype(f32) + two.astype(f32) + three.astype(f32)
    other = send(total[rows:].astype(bf16), flip_row)
    return (total[:rows] + other.astype(f32)).astype(bf16)


def across(value, blocks=4):
    rows, cols = value.shape
    piece = rows // (blocks * blocks)
    cut = value.reshape(blocks, blocks, piece, cols)
    return jnp.swapaxes(cut, 0, 1).reshape(rows, cols)


def per_device(
    tokens_a, routes_a, gates_a, tokens_b, routes_b, gates_b, grad_b, w_gate, w_up, w_down
):
    rows, quarter = tokens_a.shape
    top_k = routes_a.shape[1]
    experts = GROUPS
    capacity = min(rows, 5 * rows * top_k // (4 * experts))
    half = w_gate.shape[2] // 2
    w_gate, w_up, w_down = w_gate[0], w_up[0], w_down[0]
    core = lax.axis_index("pipe") % 2
    mine = lax.axis_index("expert")
    step = jnp.arange(4, dtype=jnp.int32)
    along_x = mine - mine % 4 + (mine + step) % 4
    along_z = (mine + 8 * step) % 32
    wanted = jnp.where(core == 0, along_x, along_z).astype(f32)

    high_a, low_a = two_parts(gates_a)
    high_b, low_b = two_parts(gates_b)
    info = sum(
        jnp.pad(part.astype(f32), ((0, 0), (i * top_k, 128 - (i + 1) * top_k)))
        for i, part in enumerate([routes_a, high_a, low_a, routes_b, high_b, low_b])
    ).astype(bf16)
    all_a = jnp.concatenate(spread(jnp.concatenate([tokens_a, info], axis=1)), axis=0)
    all_info = all_a[:, quarter:].astype(f32).T
    all_a = all_a[:, :quarter]
    spread_b = spread(jnp.concatenate([tokens_b, grad_b], axis=1))
    all_b = jnp.concatenate(spread_b, axis=0)

    count = 8 * rows
    token = jnp.arange(count, dtype=jnp.int32)
    block = token // rows
    earlier = (
        (token[:, None] < token[None, :]) & (block[:, None] == block[None, :])
    ).astype(bf16)
    size = 8 * capacity

    def picks(base):
        routes = all_info[base : base + top_k]
        gates = all_info[base + top_k : base + 2 * top_k] + all_info[base + 2 * top_k : base + 3 * top_k]
        same = routes[None, :, :] == wanted[:, None, None]
        hit = jnp.any(same, axis=1)
        gate = jnp.sum(jnp.where(same, gates[None], 0.0), axis=1)
        position = dot(hit.astype(bf16), earlier).astype(jnp.int32)
        slot = jnp.where(hit, block[None, :] * capacity + position, -1)
        chosen = slot[:, None, :] == jnp.arange(size, dtype=jnp.int32)[None, :, None]
        weighted = jnp.where(chosen, gate[:, None, :], 0.0)
        return chosen.reshape(4 * size, count), weighted.reshape(4 * size, count)

    chosen_a, weighted_a = picks(0)
    chosen_b, weighted_b = picks(3 * top_k)
    chosen_a = chosen_a.astype(bf16)
    chosen_b = chosen_b.astype(bf16)
    slot_gate_b = jnp.sum(weighted_b, axis=1, keepdims=True)

    def chunks(value):
        return [value[d * size : (d + 1) * size] for d in range(4)]

    def given(parts):
        kept, gone = [], []
        for part in parts:
            low, top = part[:, :half], part[:, half:]
            kept.append(jnp.where(core == 0, low, top))
            gone.append(jnp.where(core == 0, top, low).astype(bf16))
        got = across(send(jnp.concatenate(gone, axis=1), flip_core))
        own = jnp.concatenate(kept, axis=1) + got.astype(f32)
        return own, own.astype(bf16)

    def halves(own, far):
        total = own + far.astype(f32)
        return [total[:, i : i + half] for i in range(0, total.shape[1], half)]

    def whole(parts):
        own = jnp.concatenate(parts, axis=1)
        got = across(send(own, flip_core))
        out = []
        for i in range(len(parts)):
            a, b = own[:, i * half : (i + 1) * half], got[:, i * half : (i + 1) * half]
            out.append(
                jnp.concatenate([jnp.where(core == 0, a, b), jnp.where(core == 0, b, a)], axis=1)
            )
        return out

    pack_a = dot(chosen_a, all_a).astype(bf16)
    recv_a = exchange(after(chunks(pack_a), spread_b[3]))
    pack_b = jnp.concatenate(
        [
            dot(chosen_b, all_b[:, :quarter]).astype(bf16),
            (dot(chosen_b, all_b[:, quarter:]) * slot_gate_b).astype(bf16),
        ],
        axis=1,
    )
    recv_b = exchange(chunks(pack_b))

    xa = after(recv_a, pack_b)
    own_a, sent_a = given([dot(xa, w_gate), dot(xa, w_up)])
    far_gate_a = send(sent_a[:, :half], flip_chip)
    far_up_a = send(sent_a[:, half:], flip_chip)

    both_b = after(recv_b, far_gate_a)
    xb, gb = both_b[:, :quarter], both_b[:, quarter:]
    part_gate, part_up = dot(xb, w_gate), dot(xb, w_up)
    gb, part_gate, part_up = after((gb, part_gate, part_up), far_up_a)
    own_b, sent_b = given([part_gate, part_up, dot_t(gb, w_down)])
    far_b = send(sent_b, flip_chip)

    far_a = jnp.concatenate([far_gate_a, far_up_a], axis=1)
    gate_a, up_a = halves(own_a, after(far_a, sent_b))
    (hidden_a,) = whole([(jax.nn.silu(gate_a) * up_a).astype(bf16)])
    out_a = dot(hidden_a, w_down).astype(bf16)
    partial_a = t_dot(weighted_a.astype(bf16), exchange(chunks(out_a), back=True))

    gate_b, up_b, dh = halves(own_b, after(far_b, partial_a))
    act = jax.nn.silu(gate_b)
    hidden_b, d_gate, d_up = whole(
        [
            (act * up_b).astype(bf16),
            (dh * up_b * silu_slope(gate_b)).astype(bf16),
            (dh * act).astype(bf16),
        ]
    )
    dxb = (dot_t(d_gate, w_gate) + dot_t(d_up, w_up)).astype(bf16)
    mixed_a = gather_back(partial_a, rows, dxb)
    partial_b = t_dot(chosen_b, exchange(chunks(dxb), back=True))
    grad_tokens_b = gather_back(partial_b, rows)
    grad_gate = t_dot(xb, d_gate).astype(bf16)
    grad_up = t_dot(xb, d_up).astype(bf16)
    grad_down = t_dot(hidden_b, gb).astype(bf16)
    return (mixed_a, grad_tokens_b, grad_gate[None], grad_up[None], grad_down[None])


def solution(mesh):
    return jax.shard_map(
        per_device,
        mesh=mesh,
        in_specs=(
            P("expert", "pipe"),
            P("expert", None),
            P("expert", None),
            P("expert", "pipe"),
            P("expert", None),
            P("expert", None),
            P("expert", "pipe"),
            P("expert", "pipe", None),
            P("expert", "pipe", None),
            P("expert", None, "pipe"),
        ),
        out_specs=(
            P("expert", "pipe"),
            P("expert", "pipe"),
            P("expert", "pipe", None),
            P("expert", "pipe", None),
            P("expert", None, "pipe"),
        ),
        check_vma=False,
    )
```

```python
import functools

import jax
import jax.numpy as jnp
from jax import lax
from jax.experimental import pallas as pl
from jax.experimental.pallas import tpu as pltpu
from jax.sharding import PartitionSpec as P

BOTH = ("pipe", "expert")
PIPE = 4
GROUPS = 32
bf16 = jnp.bfloat16
f32 = jnp.float32


def after(value, *others):
    return lax.optimization_barrier((value, others))[0]


def split_place(pipe, expert):
    return pipe // 2, pipe % 2, expert // 8, (expert // 4) % 2, expert % 4


def moved(move):
    pairs = []
    for pipe in range(PIPE):
        for expert in range(GROUPS):
            yl, c, z, yh, x = move(*split_place(pipe, expert))
            target = (yl * 2 + c) * GROUPS + z * 8 + yh * 4 + x
            pairs.append((pipe * GROUPS + expert, target))
    return pairs


def send(value, move):
    return lax.ppermute(value, BOTH, moved(move))


def shift_near(d):
    def move(yl, c, z, yh, x):
        return (yl, c, (z + d) % 4, yh, x) if c == 0 else (yl, c, z, yh, (x + d) % 4)

    return move


def shift_far(d):
    def move(yl, c, z, yh, x):
        return (yl, c, z, yh, (x + d) % 4) if c == 0 else (yl, c, (z + d) % 4, yh, x)

    return move


def flip_row(yl, c, z, yh, x):
    return (yl, c, z, 1 - yh, x)


def flip_core(yl, c, z, yh, x):
    return (yl, 1 - c, z, yh, x)


def flip_chip(yl, c, z, yh, x):
    return (1 - yl, c, z, yh, x)


def dot(a, b):
    return jnp.dot(a, b, preferred_element_type=f32)


def dot_t(a, b):
    return lax.dot_general(a, b, (((1,), (1,)), ((), ())), preferred_element_type=f32)


def t_dot(a, b):
    return lax.dot_general(a, b, (((0,), (0,)), ((), ())), preferred_element_type=f32)


def silu_slope(values):
    sigma = jax.nn.sigmoid(values)
    return sigma * (1.0 + values * (1.0 - sigma))


LIGHT = pl.CostEstimate(flops=1000, bytes_accessed=1000, transcendentals=0)
ROOM = pltpu.CompilerParams(vmem_limit_bytes=48 * 1024 * 1024)
SMEM = pl.BlockSpec(memory_space=pltpu.SMEM)


def place(part, offset):
    top = part.shape[0]
    rows = lax.broadcasted_iota(jnp.int32, (top, 128), 0)
    cols = lax.broadcasted_iota(jnp.int32, (top, 128), 1)
    return t_dot(part.astype(bf16), jnp.where(cols == rows + offset, 1.0, 0.0).astype(bf16))


def payload_kernel(
    tokens_ref, tokens_b_ref, grad_b_ref, routes_a_ref, gates_a_ref, routes_b_ref, gates_b_ref,
    out_ref, out_b_ref,
):
    width = tokens_ref.shape[1]
    out_b_ref[:, :width] = tokens_b_ref[...]
    out_b_ref[:, width:] = grad_b_ref[...]
    out_ref[:, :width] = tokens_ref[...]
    info = None
    for i, (routes, gates) in enumerate(
        ((routes_a_ref, gates_a_ref), (routes_b_ref, gates_b_ref))
    ):
        top = gates.shape[0]
        high = gates[...].astype(bf16)
        low = gates[...] - high.astype(f32)
        for j, part in enumerate((routes[...].astype(f32), high, low)):
            placed = place(part, (3 * i + j) * top)
            info = placed if info is None else info + placed
    out_ref[:, width:] = info.astype(bf16)


def payload(tokens, tokens_b, grad_b, *tables):
    rows, width = tokens.shape
    return pl.pallas_call(
        payload_kernel,
        out_shape=[
            jax.ShapeDtypeStruct((rows, width + 128), bf16),
            jax.ShapeDtypeStruct((rows, 2 * width), bf16),
        ],
        cost_estimate=LIGHT,
        name="payload",
    )(tokens, tokens_b, grad_b, *[table.T for table in tables])


def one_hot(slot_ref, first, d, size):
    count = slot_ref.shape[1]
    index = lax.broadcasted_iota(jnp.int32, (size, count), 0)
    return slot_ref[first + d : first + d + 1, :] == index


def slots_of(info, wanted_ref, top, rows, capacity, slot_ref, gate_ref):
    count = info.shape[0]
    table = info.T
    hits, gates = [], []
    for i in range(2):
        base = 3 * i * top
        routes = table[base : base + top]
        gate = table[base + top : base + 2 * top] + table[base + 2 * top : base + 3 * top]
        for d in range(4):
            same = routes == wanted_ref[d].astype(f32)
            hits.append(jnp.sum(jnp.where(same, 1.0, 0.0), axis=0, keepdims=True))
            gates.append(jnp.sum(jnp.where(same, gate, 0.0), axis=0, keepdims=True))
    hit = jnp.concatenate(hits, axis=0)
    before = lax.broadcasted_iota(jnp.int32, (count, count), 0)
    token = lax.broadcasted_iota(jnp.int32, (count, count), 1)
    earlier = (before < token) & (before >= token - token % rows)
    position = dot(hit.astype(bf16), jnp.where(earlier, 1.0, 0.0).astype(bf16))
    block = lax.broadcasted_iota(jnp.int32, hit.shape, 1) // rows
    slot_ref[...] = jnp.where(hit > 0.0, block * capacity + position.astype(jnp.int32), -1)
    gate_ref[...] = jnp.concatenate(gates, axis=0)


def pack_a_kernel(top, rows, capacity, wanted_ref, *refs):
    parts, infos, outs = refs[:4], refs[4:8], refs[8:12]
    slot_ref, gate_ref, chosen = refs[12:]
    size = 8 * capacity

    @pl.when(pl.program_id(0) == 0)
    def _():
        info = jnp.concatenate([ref[...].astype(f32) for ref in infos], axis=0)
        slots_of(info, wanted_ref, top, rows, capacity, slot_ref, gate_ref)
        for d in range(4):
            chosen[d * size : (d + 1) * size, :] = jnp.where(
                one_hot(slot_ref, 0, d, size), 1.0, 0.0
            ).astype(bf16)

    values = jnp.concatenate([ref[...] for ref in parts], axis=0)
    for d in range(4):
        outs[d][...] = dot(chosen[d * size : (d + 1) * size, :], values).astype(bf16)


def pack_a(parts, wanted, top, rows, capacity, steps=2):
    pair, width = parts[0].shape
    width -= 128
    size, count = 8 * capacity, 4 * pair
    tile = width // steps
    fixed = pl.BlockSpec((8, count), lambda i: (0, 0))
    out = pl.pallas_call(
        functools.partial(pack_a_kernel, top, rows, capacity),
        grid=(steps,),
        in_specs=[SMEM]
        + [pl.BlockSpec((pair, tile), lambda i: (0, i))] * 4
        + [pl.BlockSpec((pair, 128), lambda i: (0, width // 128))] * 4,
        out_specs=[pl.BlockSpec((size, tile), lambda i: (0, i))] * 4 + [fixed] * 2,
        out_shape=[jax.ShapeDtypeStruct((size, width), bf16)] * 4
        + [jax.ShapeDtypeStruct((8, count), jnp.int32), jax.ShapeDtypeStruct((8, count), f32)],
        scratch_shapes=[pltpu.VMEM((4 * size, count), bf16)],
        compiler_params=ROOM,
        cost_estimate=LIGHT,
        name="pack_a",
    )(wanted, *parts, *parts)
    return out[:4], out[4], out[5]


def pack_b_kernel(size, half_steps, slot_ref, gate_ref, *refs):
    parts, outs = refs[:5], refs[5:9]
    chosen, weight = refs[9:]

    @pl.when(pl.program_id(0) == 0)
    def _():
        for d in range(4):
            here = one_hot(slot_ref, 4, d, size)
            chosen[d * size : (d + 1) * size, :] = jnp.where(here, 1.0, 0.0).astype(bf16)
            weight[d * size : (d + 1) * size, :] = jnp.sum(
                jnp.where(here, gate_ref[4 + d : 5 + d, :], 0.0), axis=1, keepdims=True
            )

    values = jnp.concatenate([ref[...] for ref in parts], axis=0)
    scaled = pl.program_id(0) >= half_steps
    for d in range(4):
        at = slice(d * size, (d + 1) * size)
        scale = jnp.where(scaled, weight[at, :], 1.0)
        outs[d][...] = (dot(chosen[at, :], values) * scale).astype(bf16)


def pack_b(parts, slot, gate, capacity, steps=4):
    pair, width = parts[0].shape
    size, count = 8 * capacity, 4 * pair
    tile = width // steps
    fixed = pl.BlockSpec((8, count), lambda i: (0, 0))
    return pl.pallas_call(
        functools.partial(pack_b_kernel, size, steps // 2),
        grid=(steps,),
        in_specs=[fixed] * 2 + [
            pl.BlockSpec((part.shape[0], tile), lambda i: (0, i)) for part in parts
        ],
        out_specs=[pl.BlockSpec((size, tile), lambda i: (0, i))] * 4,
        out_shape=[jax.ShapeDtypeStruct((size, width), bf16)] * 4,
        scratch_shapes=[pltpu.VMEM((4 * size, count), bf16), pltpu.VMEM((4 * size, 1), f32)],
        compiler_params=ROOM,
        cost_estimate=LIGHT,
        name="pack_b",
    )(slot, gate, *parts)


def combine_kernel(first, size, pair, slot_ref, gate_ref, *refs):
    parts, own_ref, outs, weights = refs[:4], refs[4], refs[5:8], refs[8]

    @pl.when(pl.program_id(0) == 0)
    def _():
        for d in range(4):
            here = one_hot(slot_ref, first, d, size)
            scale = gate_ref[d : d + 1, :] if first == 0 else 1.0
            weights[d * size : (d + 1) * size, :] = jnp.where(here, scale, 0.0).astype(bf16)

    values = jnp.concatenate([ref[...] for ref in parts], axis=0)
    total = t_dot(weights[...], values)
    own_ref[...] = total[:pair]
    for d in range(3):
        outs[d][...] = total[(d + 1) * pair : (d + 2) * pair].astype(bf16)


def combine(chunks, slot, gate, first, steps=2):
    size, width = chunks[0].shape
    count = slot.shape[1]
    pair = count // 4
    tile = width // steps
    fixed = pl.BlockSpec((8, count), lambda i: (0, 0))
    block = pl.BlockSpec((pair, tile), lambda i: (0, i))
    return pl.pallas_call(
        functools.partial(combine_kernel, first, size, pair),
        grid=(steps,),
        in_specs=[fixed] * 2 + [pl.BlockSpec((size, tile), lambda i: (0, i))] * 4,
        out_specs=[block] * 4,
        out_shape=[jax.ShapeDtypeStruct((pair, width), f32)]
        + [jax.ShapeDtypeStruct((pair, width), bf16)] * 3,
        scratch_shapes=[pltpu.VMEM((4 * size, count), bf16)],
        compiler_params=ROOM,
        cost_estimate=LIGHT,
        name="combine_a" if first == 0 else "combine_b",
    )(slot, gate, *chunks)


def spread(rows):
    other = send(rows, flip_row)
    pair = jnp.concatenate([rows, other], axis=0)
    far = send(pair, shift_near(2))
    up = send(pair, shift_near(1))
    down = send(pair, shift_near(3))
    return pair, up, far, down


def spread_in_steps(rows, *others):
    count = rows.shape[0]
    other = send(rows, flip_row)
    pair = after(jnp.concatenate([rows, other], axis=0), *others)
    up = send(pair, shift_near(1))
    down = send(pair, shift_near(3))
    first = send(down[:count], shift_near(3))
    last = send(up[count:], shift_near(1))
    return pair, up, first, last, down


def exchange(chunks, back=False):
    sign = -1 if back else 1
    two = send(chunks[2], shift_far(2))
    one = send(chunks[1], shift_far(sign % 4))
    three = send(chunks[3], shift_far(-sign % 4))
    return chunks[0], one, two, three


def gather_back(partials, rows, *others):
    own, one, two, three = partials
    two = send(two, shift_near(2))
    one = send(one, shift_near(3))
    three = send(three, shift_near(1))
    one, two, three = after((one, two, three), *others)
    total = own + one.astype(f32) + two.astype(f32) + three.astype(f32)
    other = send(total[rows:].astype(bf16), flip_row)
    return (total[:rows] + other.astype(f32)).astype(bf16)


def products_kernel(kinds, core_ref, *refs):
    chunks, weights = refs[:4], refs[4 : 4 + kinds]
    gone_ref, kept_ref, *inputs = refs[4 + kinds :]
    step = pl.program_id(0)
    size = chunks[0].shape[0]
    width = weights[0].shape[0]

    @pl.when(step == 0)
    def _():
        for d in range(4):
            for i, ref in enumerate(inputs):
                ref[d * size : (d + 1) * size, :] = chunks[d][:, i * width : (i + 1) * width]

    for kind in range(kinds):

        def product(kind=kind):
            if kind < 2:
                return dot(inputs[0][...], weights[kind][...])
            return dot_t(inputs[1][...], weights[kind][...])

        @pl.when(step == kind)
        def _(product=product):
            gone_ref[...] = product().astype(bf16)

        @pl.when(step == kind + kinds)
        def _(product=product):
            kept_ref[...] = product()


def products(core, chunks, weights):
    kinds = len(weights)
    size, columns = chunks[0].shape
    width, hid = weights[0].shape
    half = hid // 2
    rows = 4 * size

    def side(step, core_ref):
        return jnp.where(step < kinds, 1 - core_ref[0], core_ref[0])

    blocks = [pl.BlockSpec((width, half), lambda s, core_ref: (0, side(s, core_ref)))] * 2
    blocks += [pl.BlockSpec((half, width), lambda s, core_ref: (side(s, core_ref), 0))]
    keep = [jax.ShapeDtypeStruct((rows, width), bf16)] * (columns // width)
    return pl.pallas_call(
        functools.partial(products_kernel, kinds),
        grid_spec=pltpu.PrefetchScalarGridSpec(
            num_scalar_prefetch=1,
            grid=(2 * kinds,),
            in_specs=[pl.BlockSpec((size, columns), lambda s, core_ref: (0, 0))] * 4
            + blocks[:kinds],
            out_specs=[
                pl.BlockSpec((rows, half), lambda s, core_ref: (0, jnp.minimum(s, kinds - 1))),
                pl.BlockSpec((rows, half), lambda s, core_ref: (0, jnp.maximum(s - kinds, 0))),
            ]
            + [pl.BlockSpec((rows, width), lambda s, core_ref: (0, 0))] * len(keep),
        ),
        out_shape=[
            jax.ShapeDtypeStruct((rows, kinds * half), bf16),
            jax.ShapeDtypeStruct((rows, kinds * half), f32),
        ]
        + keep,
        compiler_params=ROOM,
        cost_estimate=LIGHT,
        name="products_a" if kinds == 2 else "products_b",
    )(core.astype(jnp.int32)[None], *chunks, *weights)


def across(value, blocks=4):
    rows, cols = value.shape
    piece = rows // (blocks * blocks)
    cut = value.reshape(blocks, blocks, piece, cols)
    return jnp.swapaxes(cut, 0, 1).reshape(rows, cols)


def per_device(
    tokens_a, routes_a, gates_a, tokens_b, routes_b, gates_b, grad_b, w_gate, w_up, w_down
):
    rows, quarter = tokens_a.shape
    top_k = routes_a.shape[1]
    experts = GROUPS
    capacity = min(rows, 5 * rows * top_k // (4 * experts))
    half = w_gate.shape[2] // 2
    w_gate, w_up, w_down = w_gate[0], w_up[0], w_down[0]
    core = lax.axis_index("pipe") % 2
    mine = lax.axis_index("expert")
    step = jnp.arange(4, dtype=jnp.int32)
    along_x = mine - mine % 4 + (mine + step) % 4
    along_z = (mine + 8 * step) % 32
    wanted = jnp.where(core == 0, along_x, along_z)

    payload_a, payload_b = payload(
        tokens_a, tokens_b, grad_b, routes_a, gates_a, routes_b, gates_b
    )
    spread_a = spread(payload_a)
    spread_b = spread_in_steps(payload_b, spread_a)
    size = 8 * capacity

    def chunks(value):
        return [value[d * size : (d + 1) * size] for d in range(4)]

    def given(gone, kept):
        own = kept + across(send(gone, flip_core)).astype(f32)
        return own, own.astype(bf16)

    def halves(own, far):
        total = own + far.astype(f32)
        return [total[:, i : i + half] for i in range(0, total.shape[1], half)]

    def whole(parts):
        own = jnp.concatenate(parts, axis=1)
        got = across(send(own, flip_core))
        out = []
        for i in range(len(parts)):
            a, b = own[:, i * half : (i + 1) * half], got[:, i * half : (i + 1) * half]
            out.append(
                jnp.concatenate([jnp.where(core == 0, a, b), jnp.where(core == 0, b, a)], axis=1)
            )
        return out

    packs_a, slot, gate = pack_a(spread_a, wanted, top_k, rows, capacity)
    recv_a = exchange(packs_a)
    packs_b = pack_b(spread_b, slot, gate, capacity)
    recv_b = exchange(packs_b)

    gone_a, kept_a, _ = products(core, after(recv_a, packs_b), [w_gate, w_up])
    own_a, sent_a = given(gone_a, kept_a)
    far_a = send(sent_a, flip_chip)

    gone_b, kept_b, xb, gb = products(core, after(recv_b, far_a), [w_gate, w_up, w_down])
    own_b, sent_b = given(gone_b, kept_b)
    far_b = send(sent_b, flip_chip)

    gate_a, up_a = halves(own_a, after(far_a, sent_b))
    (hidden_a,) = whole([(jax.nn.silu(gate_a) * up_a).astype(bf16)])
    out_a = dot(hidden_a, w_down).astype(bf16)
    partial_a = combine(exchange(chunks(out_a), back=True), slot, gate, 0)

    gate_b, up_b, dh = halves(own_b, after(far_b, partial_a))
    act = jax.nn.silu(gate_b)
    hidden_b, d_gate, d_up = whole(
        [
            (act * up_b).astype(bf16),
            (dh * up_b * silu_slope(gate_b)).astype(bf16),
            (dh * act).astype(bf16),
        ]
    )
    dxb = (dot_t(d_gate, w_gate) + dot_t(d_up, w_up)).astype(bf16)
    mixed_a = gather_back(partial_a, rows, dxb)
    partial_b = combine(exchange(chunks(dxb), back=True), slot, gate, 4)
    grad_tokens_b = gather_back(partial_b, rows)
    grad_gate = t_dot(xb, d_gate).astype(bf16)
    grad_up = t_dot(xb, d_up).astype(bf16)
    grad_down = t_dot(hidden_b, gb).astype(bf16)
    return (mixed_a, grad_tokens_b, grad_gate[None], grad_up[None], grad_down[None])


def solution(mesh):
    return jax.shard_map(
        per_device,
        mesh=mesh,
        in_specs=(
            P("expert", "pipe"),
            P("expert", None),
            P("expert", None),
            P("expert", "pipe"),
            P("expert", None),
            P("expert", None),
            P("expert", "pipe"),
            P("expert", "pipe", None),
            P("expert", "pipe", None),
            P("expert", None, "pipe"),
        ),
        out_specs=(
            P("expert", "pipe"),
            P("expert", "pipe"),
            P("expert", "pipe", None),
            P("expert", "pipe", None),
            P("expert", None, "pipe"),
        ),
        check_vma=False,
    )
```

```python
import functools

import jax
import jax.numpy as jnp
from jax import lax
from jax.experimental import pallas as pl
from jax.experimental.pallas import tpu as pltpu
from jax.sharding import PartitionSpec as P

BOTH = ("pipe", "expert")
PIPE = 4
GROUPS = 32
bf16 = jnp.bfloat16
f32 = jnp.float32


def after(value, *others):
    return lax.optimization_barrier((value, others))[0]


def split_place(pipe, expert):
    return pipe // 2, pipe % 2, expert // 8, (expert // 4) % 2, expert % 4


def moved(move):
    pairs = []
    for pipe in range(PIPE):
        for expert in range(GROUPS):
            yl, c, z, yh, x = move(*split_place(pipe, expert))
            target = (yl * 2 + c) * GROUPS + z * 8 + yh * 4 + x
            pairs.append((pipe * GROUPS + expert, target))
    return pairs


def send(value, move):
    return lax.ppermute(value, BOTH, moved(move))


def shift_near(d):
    def move(yl, c, z, yh, x):
        return (yl, c, (z + d) % 4, yh, x) if c == 0 else (yl, c, z, yh, (x + d) % 4)

    return move


def shift_far(d):
    def move(yl, c, z, yh, x):
        return (yl, c, z, yh, (x + d) % 4) if c == 0 else (yl, c, (z + d) % 4, yh, x)

    return move


def flip_row(yl, c, z, yh, x):
    return (yl, c, z, 1 - yh, x)


def flip_core(yl, c, z, yh, x):
    return (yl, 1 - c, z, yh, x)


def flip_chip(yl, c, z, yh, x):
    return (1 - yl, c, z, yh, x)


def dot(a, b):
    return jnp.dot(a, b, preferred_element_type=f32)


def dot_t(a, b):
    return lax.dot_general(a, b, (((1,), (1,)), ((), ())), preferred_element_type=f32)


def t_dot(a, b):
    return lax.dot_general(a, b, (((0,), (0,)), ((), ())), preferred_element_type=f32)


def silu_slope(values):
    sigma = jax.nn.sigmoid(values)
    return sigma * (1.0 + values * (1.0 - sigma))


LIGHT = pl.CostEstimate(flops=1000, bytes_accessed=1000, transcendentals=0)
ROOM = pltpu.CompilerParams(vmem_limit_bytes=16 * 1024 * 1024)
SMEM = pl.BlockSpec(memory_space=pltpu.SMEM)


def place(part, offset):
    top = part.shape[0]
    rows = lax.broadcasted_iota(jnp.int32, (top, 128), 0)
    cols = lax.broadcasted_iota(jnp.int32, (top, 128), 1)
    return t_dot(part.astype(bf16), jnp.where(cols == rows + offset, 1.0, 0.0).astype(bf16))


def payload_kernel(
    tokens_ref, tokens_b_ref, grad_b_ref, routes_a_ref, gates_a_ref, routes_b_ref, gates_b_ref,
    out_ref, out_b_ref,
):
    width = tokens_ref.shape[1]
    out_b_ref[:, :width] = tokens_b_ref[...]
    out_b_ref[:, width:] = grad_b_ref[...]
    out_ref[:, :width] = tokens_ref[...]
    info = None
    for i, (routes, gates) in enumerate(
        ((routes_a_ref, gates_a_ref), (routes_b_ref, gates_b_ref))
    ):
        top = gates.shape[0]
        high = gates[...].astype(bf16)
        low = gates[...] - high.astype(f32)
        for j, part in enumerate((routes[...].astype(f32), high, low)):
            placed = place(part, (3 * i + j) * top)
            info = placed if info is None else info + placed
    out_ref[:, width:] = info.astype(bf16)


def payload(tokens, tokens_b, grad_b, *tables):
    rows, width = tokens.shape
    return pl.pallas_call(
        payload_kernel,
        out_shape=[
            jax.ShapeDtypeStruct((rows, width + 128), bf16),
            jax.ShapeDtypeStruct((rows, 2 * width), bf16),
        ],
        cost_estimate=LIGHT,
        name="payload",
    )(tokens, tokens_b, grad_b, *[table.T for table in tables])


def one_hot(slot_ref, first, d, size):
    count = slot_ref.shape[1]
    index = lax.broadcasted_iota(jnp.int32, (size, count), 0)
    return slot_ref[first + d : first + d + 1, :] == index


def slots_of(info, wanted_ref, top, rows, capacity, slot_ref, gate_ref):
    count = info.shape[0]
    table = info.T
    hits, gates = [], []
    for i in range(2):
        base = 3 * i * top
        routes = table[base : base + top]
        gate = table[base + top : base + 2 * top] + table[base + 2 * top : base + 3 * top]
        for d in range(4):
            same = routes == wanted_ref[d].astype(f32)
            hits.append(jnp.sum(jnp.where(same, 1.0, 0.0), axis=0, keepdims=True))
            gates.append(jnp.sum(jnp.where(same, gate, 0.0), axis=0, keepdims=True))
    hit = jnp.concatenate(hits, axis=0)
    before = lax.broadcasted_iota(jnp.int32, (count, count), 0)
    token = lax.broadcasted_iota(jnp.int32, (count, count), 1)
    earlier = (before < token) & (before >= token - token % rows)
    position = dot(hit.astype(bf16), jnp.where(earlier, 1.0, 0.0).astype(bf16))
    block = lax.broadcasted_iota(jnp.int32, hit.shape, 1) // rows
    slot_ref[...] = jnp.where(hit > 0.0, block * capacity + position.astype(jnp.int32), -1)
    gate_ref[...] = jnp.concatenate(gates, axis=0)


def pack_a_kernel(top, rows, capacity, wanted_ref, *refs):
    parts, infos, outs = refs[:4], refs[4:8], refs[8:12]
    slot_ref, gate_ref, chosen = refs[12:]
    size = 8 * capacity

    @pl.when(pl.program_id(0) == 0)
    def _():
        info = jnp.concatenate([ref[...].astype(f32) for ref in infos], axis=0)
        slots_of(info, wanted_ref, top, rows, capacity, slot_ref, gate_ref)
        for d in range(4):
            chosen[d * size : (d + 1) * size, :] = jnp.where(
                one_hot(slot_ref, 0, d, size), 1.0, 0.0
            ).astype(bf16)

    values = jnp.concatenate([ref[...] for ref in parts], axis=0)
    for d in range(4):
        outs[d][...] = dot(chosen[d * size : (d + 1) * size, :], values).astype(bf16)


def pack_a(parts, wanted, top, rows, capacity, steps=2):
    pair, width = parts[0].shape
    width -= 128
    size, count = 8 * capacity, 4 * pair
    tile = width // steps
    fixed = pl.BlockSpec((8, count), lambda i: (0, 0))
    out = pl.pallas_call(
        functools.partial(pack_a_kernel, top, rows, capacity),
        grid=(steps,),
        in_specs=[SMEM]
        + [pl.BlockSpec((pair, tile), lambda i: (0, i))] * 4
        + [pl.BlockSpec((pair, 128), lambda i: (0, width // 128))] * 4,
        out_specs=[pl.BlockSpec((size, tile), lambda i: (0, i))] * 4 + [fixed] * 2,
        out_shape=[jax.ShapeDtypeStruct((size, width), bf16)] * 4
        + [jax.ShapeDtypeStruct((8, count), jnp.int32), jax.ShapeDtypeStruct((8, count), f32)],
        scratch_shapes=[pltpu.VMEM((4 * size, count), bf16)],
        compiler_params=ROOM,
        cost_estimate=LIGHT,
        name="pack_a",
    )(wanted, *parts, *parts)
    return out[:4], out[4], out[5]


def pack_b_kernel(size, half_steps, slot_ref, gate_ref, *refs):
    parts, outs = refs[:4], refs[4:8]
    chosen, weight = refs[8:]

    @pl.when(pl.program_id(0) == 0)
    def _():
        for d in range(4):
            here = one_hot(slot_ref, 4, d, size)
            chosen[d * size : (d + 1) * size, :] = jnp.where(here, 1.0, 0.0).astype(bf16)
            weight[d * size : (d + 1) * size, :] = jnp.sum(
                jnp.where(here, gate_ref[4 + d : 5 + d, :], 0.0), axis=1, keepdims=True
            )

    values = jnp.concatenate([ref[...] for ref in parts], axis=0)
    scaled = pl.program_id(0) >= half_steps
    for d in range(4):
        at = slice(d * size, (d + 1) * size)
        scale = jnp.where(scaled, weight[at, :], 1.0)
        outs[d][...] = (dot(chosen[at, :], values) * scale).astype(bf16)


def pack_b(parts, slot, gate, capacity, steps=4):
    pair, width = parts[0].shape
    size, count = 8 * capacity, 4 * pair
    tile = width // steps
    fixed = pl.BlockSpec((8, count), lambda i: (0, 0))
    return pl.pallas_call(
        functools.partial(pack_b_kernel, size, steps // 2),
        grid=(steps,),
        in_specs=[fixed] * 2 + [
            pl.BlockSpec((part.shape[0], tile), lambda i: (0, i)) for part in parts
        ],
        out_specs=[pl.BlockSpec((size, tile), lambda i: (0, i))] * 4,
        out_shape=[jax.ShapeDtypeStruct((size, width), bf16)] * 4,
        scratch_shapes=[pltpu.VMEM((4 * size, count), bf16), pltpu.VMEM((4 * size, 1), f32)],
        compiler_params=ROOM,
        cost_estimate=LIGHT,
        name="pack_b",
    )(slot, gate, *parts)


def combine_kernel(first, size, pair, slot_ref, gate_ref, *refs):
    parts, own_ref, outs, weights = refs[:4], refs[4], refs[5:8], refs[8]

    @pl.when(pl.program_id(0) == 0)
    def _():
        for d in range(4):
            here = one_hot(slot_ref, first, d, size)
            scale = gate_ref[d : d + 1, :] if first == 0 else 1.0
            weights[d * size : (d + 1) * size, :] = jnp.where(here, scale, 0.0).astype(bf16)

    values = jnp.concatenate([ref[...] for ref in parts], axis=0)
    total = t_dot(weights[...], values)
    own_ref[...] = total[:pair]
    for d in range(3):
        outs[d][...] = total[(d + 1) * pair : (d + 2) * pair].astype(bf16)


def combine(chunks, slot, gate, first, steps=2):
    size, width = chunks[0].shape
    count = slot.shape[1]
    pair = count // 4
    tile = width // steps
    fixed = pl.BlockSpec((8, count), lambda i: (0, 0))
    block = pl.BlockSpec((pair, tile), lambda i: (0, i))
    return pl.pallas_call(
        functools.partial(combine_kernel, first, size, pair),
        grid=(steps,),
        in_specs=[fixed] * 2 + [pl.BlockSpec((size, tile), lambda i: (0, i))] * 4,
        out_specs=[block] * 4,
        out_shape=[jax.ShapeDtypeStruct((pair, width), f32)]
        + [jax.ShapeDtypeStruct((pair, width), bf16)] * 3,
        scratch_shapes=[pltpu.VMEM((4 * size, count), bf16)],
        compiler_params=ROOM,
        cost_estimate=LIGHT,
        name="combine_a" if first == 0 else "combine_b",
    )(slot, gate, *chunks)


def spread(rows):
    other = send(rows, flip_row)
    pair = jnp.concatenate([rows, other], axis=0)
    far = send(pair, shift_near(2))
    up = send(pair, shift_near(1))
    down = send(pair, shift_near(3))
    return pair, up, far, down


def exchange(chunks, back=False):
    sign = -1 if back else 1
    two = send(chunks[2], shift_far(2))
    one = send(chunks[1], shift_far(sign % 4))
    three = send(chunks[3], shift_far(-sign % 4))
    return chunks[0], one, two, three


def gather_back(partials, rows, *others):
    own, one, two, three = partials
    two = send(two, shift_near(2))
    one = send(one, shift_near(3))
    three = send(three, shift_near(1))
    one, two, three = after((one, two, three), *others)
    total = own + one.astype(f32) + two.astype(f32) + three.astype(f32)
    other = send(total[rows:].astype(bf16), flip_row)
    return (total[:rows] + other.astype(f32)).astype(bf16)


def across(value, blocks=4):
    rows, cols = value.shape
    piece = rows // (blocks * blocks)
    cut = value.reshape(blocks, blocks, piece, cols)
    return jnp.swapaxes(cut, 0, 1).reshape(rows, cols)


def per_device(
    tokens_a, routes_a, gates_a, tokens_b, routes_b, gates_b, grad_b, w_gate, w_up, w_down
):
    rows, quarter = tokens_a.shape
    top_k = routes_a.shape[1]
    experts = GROUPS
    capacity = min(rows, 5 * rows * top_k // (4 * experts))
    half = w_gate.shape[2] // 2
    w_gate, w_up, w_down = w_gate[0], w_up[0], w_down[0]
    core = lax.axis_index("pipe") % 2
    mine = lax.axis_index("expert")
    step = jnp.arange(4, dtype=jnp.int32)
    along_x = mine - mine % 4 + (mine + step) % 4
    along_z = (mine + 8 * step) % 32
    wanted = jnp.where(core == 0, along_x, along_z)

    payload_a, payload_b = payload(
        tokens_a, tokens_b, grad_b, routes_a, gates_a, routes_b, gates_b
    )
    spread_a = spread(payload_a)
    spread_b = spread(payload_b)
    size = 8 * capacity

    def chunks(value):
        return [value[d * size : (d + 1) * size] for d in range(4)]

    def given(parts):
        kept, gone = [], []
        for part in parts:
            low, top = part[:, :half], part[:, half:]
            kept.append(jnp.where(core == 0, low, top))
            gone.append(jnp.where(core == 0, top, low).astype(bf16))
        got = across(send(jnp.concatenate(gone, axis=1), flip_core))
        own = jnp.concatenate(kept, axis=1) + got.astype(f32)
        return own, own.astype(bf16)

    def halves(own, far):
        total = own + far.astype(f32)
        return [total[:, i : i + half] for i in range(0, total.shape[1], half)]

    def whole(parts):
        own = jnp.concatenate(parts, axis=1)
        got = across(send(own, flip_core))
        out = []
        for i in range(len(parts)):
            a, b = own[:, i * half : (i + 1) * half], got[:, i * half : (i + 1) * half]
            out.append(
                jnp.concatenate([jnp.where(core == 0, a, b), jnp.where(core == 0, b, a)], axis=1)
            )
        return out

    packs_a, slot, gate = pack_a(spread_a, wanted, top_k, rows, capacity)
    recv_a = exchange(packs_a)
    packs_b = pack_b(spread_b, slot, gate, capacity)
    xa = jnp.concatenate(after(recv_a, spread_b[1], spread_b[2]), axis=0)
    own_a, sent_a = given([dot(xa, w_gate), dot(xa, w_up)])
    far_a = send(sent_a, flip_chip)

    recv_b = exchange(after(packs_b, sent_a))
    both_b = jnp.concatenate(after(recv_b, far_a), axis=0)
    xb, gb = both_b[:, :quarter], both_b[:, quarter:]
    own_b, sent_b = given([dot(xb, w_gate), dot(xb, w_up), dot_t(gb, w_down)])
    far_b = send(sent_b, flip_chip)

    gate_a, up_a = halves(own_a, after(far_a, sent_b))
    (hidden_a,) = whole([(jax.nn.silu(gate_a) * up_a).astype(bf16)])
    out_a = dot(hidden_a, w_down).astype(bf16)
    partial_a = combine(exchange(chunks(out_a), back=True), slot, gate, 0)

    gate_b, up_b, dh = halves(own_b, after(far_b, partial_a))
    act = jax.nn.silu(gate_b)
    hidden_b, d_gate, d_up = whole(
        [
            (act * up_b).astype(bf16),
            (dh * up_b * silu_slope(gate_b)).astype(bf16),
            (dh * act).astype(bf16),
        ]
    )
    dxb = (dot_t(d_gate, w_gate) + dot_t(d_up, w_up)).astype(bf16)
    mixed_a = gather_back(partial_a, rows, dxb)
    partial_b = combine(exchange(chunks(dxb), back=True), slot, gate, 4)
    grad_tokens_b = gather_back(partial_b, rows)
    grad_gate = t_dot(xb, d_gate).astype(bf16)
    grad_up = t_dot(xb, d_up).astype(bf16)
    grad_down = t_dot(hidden_b, gb).astype(bf16)
    return (mixed_a, grad_tokens_b, grad_gate[None], grad_up[None], grad_down[None])


def solution(mesh):
    return jax.shard_map(
        per_device,
        mesh=mesh,
        in_specs=(
            P("expert", "pipe"),
            P("expert", None),
            P("expert", None),
            P("expert", "pipe"),
            P("expert", None),
            P("expert", None),
            P("expert", "pipe"),
            P("expert", "pipe", None),
            P("expert", "pipe", None),
            P("expert", None, "pipe"),
        ),
        out_specs=(
            P("expert", "pipe"),
            P("expert", "pipe"),
            P("expert", "pipe", None),
            P("expert", "pipe", None),
            P("expert", None, "pipe"),
        ),
        check_vma=False,
    )
```

```python
import functools

import jax
import jax.numpy as jnp
from jax import lax
from jax.experimental import pallas as pl
from jax.experimental.pallas import tpu as pltpu
from jax.sharding import PartitionSpec as P

BOTH = ("pipe", "expert")
PIPE = 4
GROUPS = 32
bf16 = jnp.bfloat16
f32 = jnp.float32


def after(value, *others):
    return lax.optimization_barrier((value, others))[0]


def split_place(pipe, expert):
    return pipe // 2, pipe % 2, expert // 8, (expert // 4) % 2, expert % 4


def moved(move):
    pairs = []
    for pipe in range(PIPE):
        for expert in range(GROUPS):
            yl, c, z, yh, x = move(*split_place(pipe, expert))
            target = (yl * 2 + c) * GROUPS + z * 8 + yh * 4 + x
            pairs.append((pipe * GROUPS + expert, target))
    return pairs


def send(value, move):
    return lax.ppermute(value, BOTH, moved(move))


def shift_near(d):
    def move(yl, c, z, yh, x):
        return (yl, c, (z + d) % 4, yh, x) if c == 0 else (yl, c, z, yh, (x + d) % 4)

    return move


def shift_far(d):
    def move(yl, c, z, yh, x):
        return (yl, c, z, yh, (x + d) % 4) if c == 0 else (yl, c, (z + d) % 4, yh, x)

    return move


def flip_row(yl, c, z, yh, x):
    return (yl, c, z, 1 - yh, x)


def flip_core(yl, c, z, yh, x):
    return (yl, 1 - c, z, yh, x)


def flip_chip(yl, c, z, yh, x):
    return (1 - yl, c, z, yh, x)


def dot(a, b):
    return jnp.dot(a, b, preferred_element_type=f32)


def dot_t(a, b):
    return lax.dot_general(a, b, (((1,), (1,)), ((), ())), preferred_element_type=f32)


def t_dot(a, b):
    return lax.dot_general(a, b, (((0,), (0,)), ((), ())), preferred_element_type=f32)


def silu_slope(values):
    sigma = jax.nn.sigmoid(values)
    return sigma * (1.0 + values * (1.0 - sigma))


LIGHT = pl.CostEstimate(flops=1000, bytes_accessed=1000, transcendentals=0)
ROOM = pltpu.CompilerParams(vmem_limit_bytes=16 * 1024 * 1024)
SMEM = pl.BlockSpec(memory_space=pltpu.SMEM)


def place(part, offset):
    top = part.shape[0]
    rows = lax.broadcasted_iota(jnp.int32, (top, 128), 0)
    cols = lax.broadcasted_iota(jnp.int32, (top, 128), 1)
    return t_dot(part.astype(bf16), jnp.where(cols == rows + offset, 1.0, 0.0).astype(bf16))


def payload_kernel(
    tokens_ref, tokens_b_ref, grad_b_ref, routes_a_ref, gates_a_ref, routes_b_ref, gates_b_ref,
    out_ref, out_b_ref,
):
    width = tokens_ref.shape[1]
    out_b_ref[:, :width] = tokens_b_ref[...]
    out_b_ref[:, width:] = grad_b_ref[...]
    out_ref[:, :width] = tokens_ref[...]
    info = None
    for i, (routes, gates) in enumerate(
        ((routes_a_ref, gates_a_ref), (routes_b_ref, gates_b_ref))
    ):
        top = gates.shape[0]
        high = gates[...].astype(bf16)
        low = gates[...] - high.astype(f32)
        for j, part in enumerate((routes[...].astype(f32), high, low)):
            placed = place(part, (3 * i + j) * top)
            info = placed if info is None else info + placed
    out_ref[:, width:] = info.astype(bf16)


def payload(tokens, tokens_b, grad_b, *tables):
    rows, width = tokens.shape
    return pl.pallas_call(
        payload_kernel,
        out_shape=[
            jax.ShapeDtypeStruct((rows, width + 128), bf16),
            jax.ShapeDtypeStruct((rows, 2 * width), bf16),
        ],
        cost_estimate=LIGHT,
        name="payload",
    )(tokens, tokens_b, grad_b, *[table.T for table in tables])


def one_hot(slot_ref, first, d, size):
    count = slot_ref.shape[1]
    index = lax.broadcasted_iota(jnp.int32, (size, count), 0)
    return slot_ref[first + d : first + d + 1, :] == index


def slots_of(info, wanted_ref, top, rows, capacity, slot_ref, gate_ref):
    count = info.shape[0]
    table = info.T
    hits, gates = [], []
    for i in range(2):
        base = 3 * i * top
        routes = table[base : base + top]
        gate = table[base + top : base + 2 * top] + table[base + 2 * top : base + 3 * top]
        for d in range(4):
            same = routes == wanted_ref[d].astype(f32)
            hits.append(jnp.sum(jnp.where(same, 1.0, 0.0), axis=0, keepdims=True))
            gates.append(jnp.sum(jnp.where(same, gate, 0.0), axis=0, keepdims=True))
    hit = jnp.concatenate(hits, axis=0)
    before = lax.broadcasted_iota(jnp.int32, (count, count), 0)
    token = lax.broadcasted_iota(jnp.int32, (count, count), 1)
    earlier = (before < token) & (before >= token - token % rows)
    position = dot(hit.astype(bf16), jnp.where(earlier, 1.0, 0.0).astype(bf16))
    block = lax.broadcasted_iota(jnp.int32, hit.shape, 1) // rows
    slot_ref[...] = jnp.where(hit > 0.0, block * capacity + position.astype(jnp.int32), -1)
    gate_ref[...] = jnp.concatenate(gates, axis=0)


def pack_a_kernel(top, rows, capacity, wanted_ref, *refs):
    parts, infos, outs = refs[:4], refs[4:8], refs[8:12]
    slot_ref, gate_ref, chosen = refs[12:]
    size = 8 * capacity

    @pl.when(pl.program_id(0) == 0)
    def _():
        info = jnp.concatenate([ref[...].astype(f32) for ref in infos], axis=0)
        slots_of(info, wanted_ref, top, rows, capacity, slot_ref, gate_ref)
        for d in range(4):
            chosen[d * size : (d + 1) * size, :] = jnp.where(
                one_hot(slot_ref, 0, d, size), 1.0, 0.0
            ).astype(bf16)

    values = jnp.concatenate([ref[...] for ref in parts], axis=0)
    for d in range(4):
        outs[d][...] = dot(chosen[d * size : (d + 1) * size, :], values).astype(bf16)


def pack_a(parts, wanted, top, rows, capacity, steps=2):
    pair, width = parts[0].shape
    width -= 128
    size, count = 8 * capacity, 4 * pair
    tile = width // steps
    fixed = pl.BlockSpec((8, count), lambda i: (0, 0))
    out = pl.pallas_call(
        functools.partial(pack_a_kernel, top, rows, capacity),
        grid=(steps,),
        in_specs=[SMEM]
        + [pl.BlockSpec((pair, tile), lambda i: (0, i))] * 4
        + [pl.BlockSpec((pair, 128), lambda i: (0, width // 128))] * 4,
        out_specs=[pl.BlockSpec((size, tile), lambda i: (0, i))] * 4 + [fixed] * 2,
        out_shape=[jax.ShapeDtypeStruct((size, width), bf16)] * 4
        + [jax.ShapeDtypeStruct((8, count), jnp.int32), jax.ShapeDtypeStruct((8, count), f32)],
        scratch_shapes=[pltpu.VMEM((4 * size, count), bf16)],
        compiler_params=ROOM,
        cost_estimate=LIGHT,
        name="pack_a",
    )(wanted, *parts, *parts)
    return out[:4], out[4], out[5]


def pack_b_kernel(size, half_steps, slot_ref, gate_ref, *refs):
    parts, outs = refs[:4], refs[4:8]
    chosen, weight = refs[8:]

    @pl.when(pl.program_id(0) == 0)
    def _():
        for d in range(4):
            here = one_hot(slot_ref, 4, d, size)
            chosen[d * size : (d + 1) * size, :] = jnp.where(here, 1.0, 0.0).astype(bf16)
            weight[d * size : (d + 1) * size, :] = jnp.sum(
                jnp.where(here, gate_ref[4 + d : 5 + d, :], 0.0), axis=1, keepdims=True
            )

    values = jnp.concatenate([ref[...] for ref in parts], axis=0)
    scaled = pl.program_id(0) >= half_steps
    for d in range(4):
        at = slice(d * size, (d + 1) * size)
        scale = jnp.where(scaled, weight[at, :], 1.0)
        outs[d][...] = (dot(chosen[at, :], values) * scale).astype(bf16)


def pack_b(parts, slot, gate, capacity, steps=4):
    pair, width = parts[0].shape
    size, count = 8 * capacity, 4 * pair
    tile = width // steps
    fixed = pl.BlockSpec((8, count), lambda i: (0, 0))
    return pl.pallas_call(
        functools.partial(pack_b_kernel, size, steps // 2),
        grid=(steps,),
        in_specs=[fixed] * 2 + [
            pl.BlockSpec((part.shape[0], tile), lambda i: (0, i)) for part in parts
        ],
        out_specs=[pl.BlockSpec((size, tile), lambda i: (0, i))] * 4,
        out_shape=[jax.ShapeDtypeStruct((size, width), bf16)] * 4,
        scratch_shapes=[pltpu.VMEM((4 * size, count), bf16), pltpu.VMEM((4 * size, 1), f32)],
        compiler_params=ROOM,
        cost_estimate=LIGHT,
        name="pack_b",
    )(slot, gate, *parts)


def combine_kernel(first, size, pair, slot_ref, gate_ref, *refs):
    parts, own_ref, outs, weights = refs[:4], refs[4], refs[5:8], refs[8]

    @pl.when(pl.program_id(0) == 0)
    def _():
        for d in range(4):
            here = one_hot(slot_ref, first, d, size)
            scale = gate_ref[d : d + 1, :] if first == 0 else 1.0
            weights[d * size : (d + 1) * size, :] = jnp.where(here, scale, 0.0).astype(bf16)

    values = jnp.concatenate([ref[...] for ref in parts], axis=0)
    total = t_dot(weights[...], values)
    own_ref[...] = total[:pair]
    for d in range(3):
        outs[d][...] = total[(d + 1) * pair : (d + 2) * pair].astype(bf16)


def combine(chunks, slot, gate, first, steps=2):
    size, width = chunks[0].shape
    count = slot.shape[1]
    pair = count // 4
    tile = width // steps
    fixed = pl.BlockSpec((8, count), lambda i: (0, 0))
    block = pl.BlockSpec((pair, tile), lambda i: (0, i))
    return pl.pallas_call(
        functools.partial(combine_kernel, first, size, pair),
        grid=(steps,),
        in_specs=[fixed] * 2 + [pl.BlockSpec((size, tile), lambda i: (0, i))] * 4,
        out_specs=[block] * 4,
        out_shape=[jax.ShapeDtypeStruct((pair, width), f32)]
        + [jax.ShapeDtypeStruct((pair, width), bf16)] * 3,
        scratch_shapes=[pltpu.VMEM((4 * size, count), bf16)],
        compiler_params=ROOM,
        cost_estimate=LIGHT,
        name="combine_a" if first == 0 else "combine_b",
    )(slot, gate, *chunks)


def spread(rows):
    other = send(rows, flip_row)
    pair = jnp.concatenate([rows, other], axis=0)
    far = send(pair, shift_near(2))
    up = send(pair, shift_near(1))
    down = send(pair, shift_near(3))
    return pair, up, far, down


def exchange(chunks, back=False):
    sign = -1 if back else 1
    two = send(chunks[2], shift_far(2))
    one = send(chunks[1], shift_far(sign % 4))
    three = send(chunks[3], shift_far(-sign % 4))
    return chunks[0], one, two, three


def gather_back(partials):
    own, one, two, three = partials
    two = send(two, shift_near(2))
    one = send(one, shift_near(3))
    three = send(three, shift_near(1))
    return own + one.astype(f32) + two.astype(f32) + three.astype(f32)


def finish(total, rows):
    other = send(total[rows:].astype(bf16), flip_row)
    return (total[:rows] + other.astype(f32)).astype(bf16)


def across(value, blocks=4):
    rows, cols = value.shape
    piece = rows // (blocks * blocks)
    cut = value.reshape(blocks, blocks, piece, cols)
    return jnp.swapaxes(cut, 0, 1).reshape(rows, cols)


def per_device(
    tokens_a, routes_a, gates_a, tokens_b, routes_b, gates_b, grad_b, w_gate, w_up, w_down
):
    rows, quarter = tokens_a.shape
    top_k = routes_a.shape[1]
    experts = GROUPS
    capacity = min(rows, 5 * rows * top_k // (4 * experts))
    half = w_gate.shape[2] // 2
    w_gate, w_up, w_down = w_gate[0], w_up[0], w_down[0]
    core = lax.axis_index("pipe") % 2
    mine = lax.axis_index("expert")
    step = jnp.arange(4, dtype=jnp.int32)
    along_x = mine - mine % 4 + (mine + step) % 4
    along_z = (mine + 8 * step) % 32
    wanted = jnp.where(core == 0, along_x, along_z)

    payload_a, payload_b = payload(
        tokens_a, tokens_b, grad_b, routes_a, gates_a, routes_b, gates_b
    )
    spread_a = spread(payload_a)
    spread_b = spread(payload_b)
    size = 8 * capacity

    def chunks(value):
        return [value[d * size : (d + 1) * size] for d in range(4)]

    def given(parts):
        kept, gone = [], []
        for part in parts:
            low, top = part[:, :half], part[:, half:]
            kept.append(jnp.where(core == 0, low, top))
            gone.append(jnp.where(core == 0, top, low).astype(bf16))
        got = across(send(jnp.concatenate(gone, axis=1), flip_core))
        own = jnp.concatenate(kept, axis=1) + got.astype(f32)
        return own, own.astype(bf16)

    def halves(own, far):
        total = own + far.astype(f32)
        return [total[:, i : i + half] for i in range(0, total.shape[1], half)]

    def whole(parts):
        own = jnp.concatenate(parts, axis=1)
        got = across(send(own, flip_core))
        out = []
        for i in range(len(parts)):
            a, b = own[:, i * half : (i + 1) * half], got[:, i * half : (i + 1) * half]
            out.append(
                jnp.concatenate([jnp.where(core == 0, a, b), jnp.where(core == 0, b, a)], axis=1)
            )
        return out

    packs_a, slot, gate = pack_a(spread_a, wanted, top_k, rows, capacity)
    recv_a = exchange(after(packs_a, spread_b[3]))
    packs_b = pack_b(spread_b, slot, gate, capacity)
    xa = jnp.concatenate(after(recv_a, packs_b), axis=0)
    own_a, sent_a = given([dot(xa, w_gate), dot(xa, w_up)])
    far_a = send(sent_a, flip_chip)

    recv_b = exchange(after(packs_b, sent_a))
    both_b = jnp.concatenate(after(recv_b, far_a), axis=0)
    xb, gb = both_b[:, :quarter], both_b[:, quarter:]
    own_b, sent_b = given([dot(xb, w_gate), dot(xb, w_up), dot_t(gb, w_down)])
    far_b = send(sent_b, flip_chip)

    gate_a, up_a = halves(own_a, after(far_a, sent_b))
    (hidden_a,) = whole([(jax.nn.silu(gate_a) * up_a).astype(bf16)])
    out_a = dot(hidden_a, w_down).astype(bf16)
    partial_a = combine(exchange(chunks(out_a), back=True), slot, gate, 0)

    total_a = gather_back(partial_a)
    gate_b, up_b, dh = halves(own_b, after(far_b, total_a))
    act = jax.nn.silu(gate_b)
    hidden_b, d_gate, d_up = whole(
        [
            (act * up_b).astype(bf16),
            (dh * up_b * silu_slope(gate_b)).astype(bf16),
            (dh * act).astype(bf16),
        ]
    )
    dxb = (dot_t(d_gate, w_gate) + dot_t(d_up, w_up)).astype(bf16)
    mixed_a = finish(total_a, rows)
    partial_b = combine(exchange(chunks(dxb), back=True), slot, gate, 4)
    grad_tokens_b = finish(gather_back(partial_b), rows)
    grad_gate = t_dot(xb, d_gate).astype(bf16)
    grad_up = t_dot(xb, d_up).astype(bf16)
    grad_down = t_dot(hidden_b, gb).astype(bf16)
    return (mixed_a, grad_tokens_b, grad_gate[None], grad_up[None], grad_down[None])


def solution(mesh):
    return jax.shard_map(
        per_device,
        mesh=mesh,
        in_specs=(
            P("expert", "pipe"),
            P("expert", None),
            P("expert", None),
            P("expert", "pipe"),
            P("expert", None),
            P("expert", None),
            P("expert", "pipe"),
            P("expert", "pipe", None),
            P("expert", "pipe", None),
            P("expert", None, "pipe"),
        ),
        out_specs=(
            P("expert", "pipe"),
            P("expert", "pipe"),
            P("expert", "pipe", None),
            P("expert", "pipe", None),
            P("expert", None, "pipe"),
        ),
        check_vma=False,
    )
```

```python
import functools

import jax
import jax.numpy as jnp
from jax import lax
from jax.experimental import pallas as pl
from jax.experimental.pallas import tpu as pltpu
from jax.sharding import PartitionSpec as P

BOTH = ("pipe", "expert")
PIPE = 4
GROUPS = 32
bf16 = jnp.bfloat16
f32 = jnp.float32


def after(value, *others):
    return lax.optimization_barrier((value, others))[0]


def split_place(pipe, expert):
    return pipe // 2, pipe % 2, expert // 8, (expert // 4) % 2, expert % 4


def moved(move):
    pairs = []
    for pipe in range(PIPE):
        for expert in range(GROUPS):
            yl, c, z, yh, x = move(*split_place(pipe, expert))
            target = (yl * 2 + c) * GROUPS + z * 8 + yh * 4 + x
            pairs.append((pipe * GROUPS + expert, target))
    return pairs


def send(value, move):
    return lax.ppermute(value, BOTH, moved(move))


def shift_near(d):
    def move(yl, c, z, yh, x):
        return (yl, c, (z + d) % 4, yh, x) if c == 0 else (yl, c, z, yh, (x + d) % 4)

    return move


def shift_far(d):
    def move(yl, c, z, yh, x):
        return (yl, c, z, yh, (x + d) % 4) if c == 0 else (yl, c, (z + d) % 4, yh, x)

    return move


def flip_row(yl, c, z, yh, x):
    return (yl, c, z, 1 - yh, x)


def flip_core(yl, c, z, yh, x):
    return (yl, 1 - c, z, yh, x)


def flip_chip(yl, c, z, yh, x):
    return (1 - yl, c, z, yh, x)


def dot(a, b):
    return jnp.dot(a, b, preferred_element_type=f32)


def dot_t(a, b):
    return lax.dot_general(a, b, (((1,), (1,)), ((), ())), preferred_element_type=f32)


def t_dot(a, b):
    return lax.dot_general(a, b, (((0,), (0,)), ((), ())), preferred_element_type=f32)


def silu_slope(values):
    sigma = jax.nn.sigmoid(values)
    return sigma * (1.0 + values * (1.0 - sigma))


LIGHT = pl.CostEstimate(flops=1000, bytes_accessed=1000, transcendentals=0)
ROOM = pltpu.CompilerParams(vmem_limit_bytes=16 * 1024 * 1024)
SMEM = pl.BlockSpec(memory_space=pltpu.SMEM)


def place(part, offset):
    top = part.shape[0]
    rows = lax.broadcasted_iota(jnp.int32, (top, 128), 0)
    cols = lax.broadcasted_iota(jnp.int32, (top, 128), 1)
    return t_dot(part.astype(bf16), jnp.where(cols == rows + offset, 1.0, 0.0).astype(bf16))


def payload_kernel(
    tokens_ref, tokens_b_ref, grad_b_ref, routes_a_ref, gates_a_ref, routes_b_ref, gates_b_ref,
    out_ref, out_b_ref,
):
    width = tokens_ref.shape[1]
    out_b_ref[:, :width] = tokens_b_ref[...]
    out_b_ref[:, width:] = grad_b_ref[...]
    out_ref[:, :width] = tokens_ref[...]
    info = None
    for i, (routes, gates) in enumerate(
        ((routes_a_ref, gates_a_ref), (routes_b_ref, gates_b_ref))
    ):
        top = gates.shape[0]
        high = gates[...].astype(bf16)
        low = gates[...] - high.astype(f32)
        for j, part in enumerate((routes[...].astype(f32), high, low)):
            placed = place(part, (3 * i + j) * top)
            info = placed if info is None else info + placed
    out_ref[:, width:] = info.astype(bf16)


def payload(tokens, tokens_b, grad_b, *tables):
    rows, width = tokens.shape
    return pl.pallas_call(
        payload_kernel,
        out_shape=[
            jax.ShapeDtypeStruct((rows, width + 128), bf16),
            jax.ShapeDtypeStruct((rows, 2 * width), bf16),
        ],
        cost_estimate=LIGHT,
        name="payload",
    )(tokens, tokens_b, grad_b, *[table.T for table in tables])


def one_hot(slot_ref, first, d, size):
    count = slot_ref.shape[1]
    index = lax.broadcasted_iota(jnp.int32, (size, count), 0)
    return slot_ref[first + d : first + d + 1, :] == index


def slots_of(info, wanted_ref, top, rows, capacity, slot_ref, gate_ref):
    count = info.shape[0]
    table = info.T
    hits, gates = [], []
    for i in range(2):
        base = 3 * i * top
        routes = table[base : base + top]
        gate = table[base + top : base + 2 * top] + table[base + 2 * top : base + 3 * top]
        for d in range(4):
            same = routes == wanted_ref[d].astype(f32)
            hits.append(jnp.sum(jnp.where(same, 1.0, 0.0), axis=0, keepdims=True))
            gates.append(jnp.sum(jnp.where(same, gate, 0.0), axis=0, keepdims=True))
    hit = jnp.concatenate(hits, axis=0)
    before = lax.broadcasted_iota(jnp.int32, (count, count), 0)
    token = lax.broadcasted_iota(jnp.int32, (count, count), 1)
    earlier = (before < token) & (before >= token - token % rows)
    position = dot(hit.astype(bf16), jnp.where(earlier, 1.0, 0.0).astype(bf16))
    block = lax.broadcasted_iota(jnp.int32, hit.shape, 1) // rows
    slot_ref[...] = jnp.where(hit > 0.0, block * capacity + position.astype(jnp.int32), -1)
    gate_ref[...] = jnp.concatenate(gates, axis=0)


def pack_a_kernel(top, rows, capacity, wanted_ref, *refs):
    parts, infos, outs = refs[:4], refs[4:8], refs[8:12]
    slot_ref, gate_ref, chosen = refs[12:]
    size = 8 * capacity

    @pl.when(pl.program_id(0) == 0)
    def _():
        info = jnp.concatenate([ref[...].astype(f32) for ref in infos], axis=0)
        slots_of(info, wanted_ref, top, rows, capacity, slot_ref, gate_ref)
        for d in range(4):
            chosen[d * size : (d + 1) * size, :] = jnp.where(
                one_hot(slot_ref, 0, d, size), 1.0, 0.0
            ).astype(bf16)

    values = jnp.concatenate([ref[...] for ref in parts], axis=0)
    for d in range(4):
        outs[d][...] = dot(chosen[d * size : (d + 1) * size, :], values).astype(bf16)


def pack_a(parts, wanted, top, rows, capacity, steps=2):
    pair, width = parts[0].shape
    width -= 128
    size, count = 8 * capacity, 4 * pair
    tile = width // steps
    fixed = pl.BlockSpec((8, count), lambda i: (0, 0))
    out = pl.pallas_call(
        functools.partial(pack_a_kernel, top, rows, capacity),
        grid=(steps,),
        in_specs=[SMEM]
        + [pl.BlockSpec((pair, tile), lambda i: (0, i))] * 4
        + [pl.BlockSpec((pair, 128), lambda i: (0, width // 128))] * 4,
        out_specs=[pl.BlockSpec((size, tile), lambda i: (0, i))] * 4 + [fixed] * 2,
        out_shape=[jax.ShapeDtypeStruct((size, width), bf16)] * 4
        + [jax.ShapeDtypeStruct((8, count), jnp.int32), jax.ShapeDtypeStruct((8, count), f32)],
        scratch_shapes=[pltpu.VMEM((4 * size, count), bf16)],
        compiler_params=ROOM,
        cost_estimate=LIGHT,
        name="pack_a",
    )(wanted, *parts, *parts)
    return out[:4], out[4], out[5]


def pack_b_kernel(size, half_steps, slot_ref, gate_ref, *refs):
    parts, outs = refs[:5], refs[5:9]
    chosen, weight = refs[9:]

    @pl.when(pl.program_id(0) == 0)
    def _():
        for d in range(4):
            here = one_hot(slot_ref, 4, d, size)
            chosen[d * size : (d + 1) * size, :] = jnp.where(here, 1.0, 0.0).astype(bf16)
            weight[d * size : (d + 1) * size, :] = jnp.sum(
                jnp.where(here, gate_ref[4 + d : 5 + d, :], 0.0), axis=1, keepdims=True
            )

    values = jnp.concatenate([ref[...] for ref in parts], axis=0)
    scaled = pl.program_id(0) >= half_steps
    for d in range(4):
        at = slice(d * size, (d + 1) * size)
        scale = jnp.where(scaled, weight[at, :], 1.0)
        outs[d][...] = (dot(chosen[at, :], values) * scale).astype(bf16)


def pack_b(parts, slot, gate, capacity, steps=4):
    pair, width = parts[0].shape
    size, count = 8 * capacity, 4 * pair
    tile = width // steps
    fixed = pl.BlockSpec((8, count), lambda i: (0, 0))
    return pl.pallas_call(
        functools.partial(pack_b_kernel, size, steps // 2),
        grid=(steps,),
        in_specs=[fixed] * 2 + [
            pl.BlockSpec((part.shape[0], tile), lambda i: (0, i)) for part in parts
        ],
        out_specs=[pl.BlockSpec((size, tile), lambda i: (0, i))] * 4,
        out_shape=[jax.ShapeDtypeStruct((size, width), bf16)] * 4,
        scratch_shapes=[pltpu.VMEM((4 * size, count), bf16), pltpu.VMEM((4 * size, 1), f32)],
        compiler_params=ROOM,
        cost_estimate=LIGHT,
        name="pack_b",
    )(slot, gate, *parts)


def combine_kernel(first, size, pair, slot_ref, gate_ref, *refs):
    parts, own_ref, outs, weights = refs[:4], refs[4], refs[5:8], refs[8]

    @pl.when(pl.program_id(0) == 0)
    def _():
        for d in range(4):
            here = one_hot(slot_ref, first, d, size)
            scale = gate_ref[d : d + 1, :] if first == 0 else 1.0
            weights[d * size : (d + 1) * size, :] = jnp.where(here, scale, 0.0).astype(bf16)

    values = jnp.concatenate([ref[...] for ref in parts], axis=0)
    total = t_dot(weights[...], values)
    own_ref[...] = total[:pair]
    for d in range(3):
        outs[d][...] = total[(d + 1) * pair : (d + 2) * pair].astype(bf16)


def combine(chunks, slot, gate, first, steps=2):
    size, width = chunks[0].shape
    count = slot.shape[1]
    pair = count // 4
    tile = width // steps
    fixed = pl.BlockSpec((8, count), lambda i: (0, 0))
    block = pl.BlockSpec((pair, tile), lambda i: (0, i))
    return pl.pallas_call(
        functools.partial(combine_kernel, first, size, pair),
        grid=(steps,),
        in_specs=[fixed] * 2 + [pl.BlockSpec((size, tile), lambda i: (0, i))] * 4,
        out_specs=[block] * 4,
        out_shape=[jax.ShapeDtypeStruct((pair, width), f32)]
        + [jax.ShapeDtypeStruct((pair, width), bf16)] * 3,
        scratch_shapes=[pltpu.VMEM((4 * size, count), bf16)],
        compiler_params=ROOM,
        cost_estimate=LIGHT,
        name="combine_a" if first == 0 else "combine_b",
    )(slot, gate, *chunks)


def row_pair(rows):
    return jnp.concatenate([rows, send(rows, flip_row)], axis=0)


def spread(pair):
    far = send(pair, shift_near(2))
    up = send(pair, shift_near(1))
    down = send(pair, shift_near(3))
    return pair, up, far, down


def spread_in_steps(pair):
    rows = pair.shape[0] // 2
    up = send(pair, shift_near(1))
    down = send(pair, shift_near(3))
    first = send(down[:rows], shift_near(3))
    last = send(up[rows:], shift_near(1))
    return pair, up, first, last, down


def exchange(chunks, back=False):
    sign = -1 if back else 1
    two = send(chunks[2], shift_far(2))
    one = send(chunks[1], shift_far(sign % 4))
    three = send(chunks[3], shift_far(-sign % 4))
    return chunks[0], one, two, three


def gather_back(partials):
    own, one, two, three = partials
    two = send(two, shift_near(2))
    one = send(one, shift_near(3))
    three = send(three, shift_near(1))
    return own + one.astype(f32) + two.astype(f32) + three.astype(f32)


def finish(total, rows):
    other = send(total[rows:].astype(bf16), flip_row)
    return (total[:rows] + other.astype(f32)).astype(bf16)


def across(value, blocks=4):
    rows, cols = value.shape
    piece = rows // (blocks * blocks)
    cut = value.reshape(blocks, blocks, piece, cols)
    return jnp.swapaxes(cut, 0, 1).reshape(rows, cols)


def per_device(
    tokens_a, routes_a, gates_a, tokens_b, routes_b, gates_b, grad_b, w_gate, w_up, w_down
):
    rows, quarter = tokens_a.shape
    top_k = routes_a.shape[1]
    experts = GROUPS
    capacity = min(rows, 5 * rows * top_k // (4 * experts))
    half = w_gate.shape[2] // 2
    w_gate, w_up, w_down = w_gate[0], w_up[0], w_down[0]
    core = lax.axis_index("pipe") % 2
    mine = lax.axis_index("expert")
    step = jnp.arange(4, dtype=jnp.int32)
    along_x = mine - mine % 4 + (mine + step) % 4
    along_z = (mine + 8 * step) % 32
    wanted = jnp.where(core == 0, along_x, along_z)

    payload_a, payload_b = payload(
        tokens_a, tokens_b, grad_b, routes_a, gates_a, routes_b, gates_b
    )
    pair_a, pair_b = row_pair(payload_a), row_pair(payload_b)
    spread_a = spread(pair_a)
    size = 8 * capacity

    def chunks(value):
        return [value[d * size : (d + 1) * size] for d in range(4)]

    def given(parts):
        kept, gone = [], []
        for part in parts:
            low, top = part[:, :half], part[:, half:]
            kept.append(jnp.where(core == 0, low, top))
            gone.append(jnp.where(core == 0, top, low).astype(bf16))
        got = across(send(jnp.concatenate(gone, axis=1), flip_core))
        own = jnp.concatenate(kept, axis=1) + got.astype(f32)
        return own, own.astype(bf16)

    def halves(own, far):
        total = own + far.astype(f32)
        return [total[:, i : i + half] for i in range(0, total.shape[1], half)]

    def whole(parts):
        own = jnp.concatenate(parts, axis=1)
        got = across(send(own, flip_core))
        out = []
        for i in range(len(parts)):
            a, b = own[:, i * half : (i + 1) * half], got[:, i * half : (i + 1) * half]
            out.append(
                jnp.concatenate([jnp.where(core == 0, a, b), jnp.where(core == 0, b, a)], axis=1)
            )
        return out

    wanted = after(wanted, pair_b)
    packs_a, slot, gate = pack_a(spread_a, wanted, top_k, rows, capacity)
    recv_a = exchange(packs_a)
    spread_b = spread_in_steps(after(pair_b, slot))
    packs_b = pack_b(spread_b, slot, gate, capacity)

    xa = jnp.concatenate(after(recv_a, spread_b[1], spread_b[4]), axis=0)
    own_a, sent_a = given([dot(xa, w_gate), dot(xa, w_up)])
    far_a = send(sent_a, flip_chip)

    recv_b = exchange(after(packs_b, sent_a))
    both_b = jnp.concatenate(after(recv_b, far_a), axis=0)
    xb, gb = both_b[:, :quarter], both_b[:, quarter:]
    own_b, sent_b = given([dot(xb, w_gate), dot(xb, w_up), dot_t(gb, w_down)])
    far_b = send(sent_b, flip_chip)

    gate_a, up_a = halves(own_a, after(far_a, sent_b))
    (hidden_a,) = whole([(jax.nn.silu(gate_a) * up_a).astype(bf16)])
    out_a = dot(hidden_a, w_down).astype(bf16)
    partial_a = combine(exchange(chunks(out_a), back=True), slot, gate, 0)

    total_a = gather_back(partial_a)
    gate_b, up_b, dh = halves(own_b, after(far_b, total_a))
    act = jax.nn.silu(gate_b)
    hidden_b, d_gate, d_up = whole(
        [
            (act * up_b).astype(bf16),
            (dh * up_b * silu_slope(gate_b)).astype(bf16),
            (dh * act).astype(bf16),
        ]
    )
    dxb = (dot_t(d_gate, w_gate) + dot_t(d_up, w_up)).astype(bf16)
    back_b = exchange(chunks(dxb), back=True)
    mixed_a = finish(after(total_a, dxb), rows)
    grad_tokens_b = finish(gather_back(combine(back_b, slot, gate, 4)), rows)
    grad_gate = t_dot(xb, d_gate).astype(bf16)
    grad_up = t_dot(xb, d_up).astype(bf16)
    grad_down = t_dot(hidden_b, gb).astype(bf16)
    return (mixed_a, grad_tokens_b, grad_gate[None], grad_up[None], grad_down[None])


def solution(mesh):
    return jax.shard_map(
        per_device,
        mesh=mesh,
        in_specs=(
            P("expert", "pipe"),
            P("expert", None),
            P("expert", None),
            P("expert", "pipe"),
            P("expert", None),
            P("expert", None),
            P("expert", "pipe"),
            P("expert", "pipe", None),
            P("expert", "pipe", None),
            P("expert", None, "pipe"),
        ),
        out_specs=(
            P("expert", "pipe"),
            P("expert", "pipe"),
            P("expert", "pipe", None),
            P("expert", "pipe", None),
            P("expert", None, "pipe"),
        ),
        check_vma=False,
    )
```

```python
import functools

import jax
import jax.numpy as jnp
from jax import lax
from jax.experimental import pallas as pl
from jax.experimental.pallas import tpu as pltpu
from jax.sharding import PartitionSpec as P

BOTH = ("pipe", "expert")
PIPE = 4
GROUPS = 32
bf16 = jnp.bfloat16
f32 = jnp.float32


def after(value, *others):
    return lax.optimization_barrier((value, others))[0]


def split_place(pipe, expert):
    return pipe // 2, pipe % 2, expert // 8, (expert // 4) % 2, expert % 4


def moved(move):
    pairs = []
    for pipe in range(PIPE):
        for expert in range(GROUPS):
            yl, c, z, yh, x = move(*split_place(pipe, expert))
            target = (yl * 2 + c) * GROUPS + z * 8 + yh * 4 + x
            pairs.append((pipe * GROUPS + expert, target))
    return pairs


def send(value, move):
    return lax.ppermute(value, BOTH, moved(move))


def shift_near(d):
    def move(yl, c, z, yh, x):
        return (yl, c, (z + d) % 4, yh, x) if c == 0 else (yl, c, z, yh, (x + d) % 4)

    return move


def shift_far(d):
    def move(yl, c, z, yh, x):
        return (yl, c, z, yh, (x + d) % 4) if c == 0 else (yl, c, (z + d) % 4, yh, x)

    return move


def flip_row(yl, c, z, yh, x):
    return (yl, c, z, 1 - yh, x)


def flip_core(yl, c, z, yh, x):
    return (yl, 1 - c, z, yh, x)


def flip_chip(yl, c, z, yh, x):
    return (1 - yl, c, z, yh, x)


def dot(a, b):
    return jnp.dot(a, b, preferred_element_type=f32)


def dot_t(a, b):
    return lax.dot_general(a, b, (((1,), (1,)), ((), ())), preferred_element_type=f32)


def t_dot(a, b):
    return lax.dot_general(a, b, (((0,), (0,)), ((), ())), preferred_element_type=f32)


def silu_slope(values):
    sigma = jax.nn.sigmoid(values)
    return sigma * (1.0 + values * (1.0 - sigma))


LIGHT = pl.CostEstimate(flops=1000, bytes_accessed=1000, transcendentals=0)
ROOM = pltpu.CompilerParams(vmem_limit_bytes=16 * 1024 * 1024)
SMEM = pl.BlockSpec(memory_space=pltpu.SMEM)


def place(part, offset):
    top = part.shape[0]
    rows = lax.broadcasted_iota(jnp.int32, (top, 128), 0)
    cols = lax.broadcasted_iota(jnp.int32, (top, 128), 1)
    return t_dot(part.astype(bf16), jnp.where(cols == rows + offset, 1.0, 0.0).astype(bf16))


def payload_kernel(
    tokens_ref, tokens_b_ref, grad_b_ref, routes_a_ref, gates_a_ref, routes_b_ref, gates_b_ref,
    out_ref, out_b_ref,
):
    width = tokens_ref.shape[1]
    out_b_ref[:, :width] = tokens_b_ref[...]
    out_b_ref[:, width:] = grad_b_ref[...]
    out_ref[:, :width] = tokens_ref[...]
    info = None
    for i, (routes, gates) in enumerate(
        ((routes_a_ref, gates_a_ref), (routes_b_ref, gates_b_ref))
    ):
        top = gates.shape[0]
        high = gates[...].astype(bf16)
        low = gates[...] - high.astype(f32)
        for j, part in enumerate((routes[...].astype(f32), high, low)):
            placed = place(part, (3 * i + j) * top)
            info = placed if info is None else info + placed
    out_ref[:, width:] = info.astype(bf16)


def payload(tokens, tokens_b, grad_b, *tables):
    rows, width = tokens.shape
    return pl.pallas_call(
        payload_kernel,
        out_shape=[
            jax.ShapeDtypeStruct((rows, width + 128), bf16),
            jax.ShapeDtypeStruct((rows, 2 * width), bf16),
        ],
        cost_estimate=LIGHT,
        name="payload",
    )(tokens, tokens_b, grad_b, *[table.T for table in tables])


def one_hot(slot_ref, first, d, size):
    count = slot_ref.shape[1]
    index = lax.broadcasted_iota(jnp.int32, (size, count), 0)
    return slot_ref[first + d : first + d + 1, :] == index


def slots_of(info, wanted_ref, top, rows, capacity, slot_ref, gate_ref):
    count = info.shape[0]
    table = info.T
    hits, gates = [], []
    for i in range(2):
        base = 3 * i * top
        routes = table[base : base + top]
        gate = table[base + top : base + 2 * top] + table[base + 2 * top : base + 3 * top]
        for d in range(4):
            same = routes == wanted_ref[d].astype(f32)
            hits.append(jnp.sum(jnp.where(same, 1.0, 0.0), axis=0, keepdims=True))
            gates.append(jnp.sum(jnp.where(same, gate, 0.0), axis=0, keepdims=True))
    hit = jnp.concatenate(hits, axis=0)
    before = lax.broadcasted_iota(jnp.int32, (count, count), 0)
    token = lax.broadcasted_iota(jnp.int32, (count, count), 1)
    earlier = (before < token) & (before >= token - token % rows)
    position = dot(hit.astype(bf16), jnp.where(earlier, 1.0, 0.0).astype(bf16))
    block = lax.broadcasted_iota(jnp.int32, hit.shape, 1) // rows
    slot_ref[...] = jnp.where(hit > 0.0, block * capacity + position.astype(jnp.int32), -1)
    gate_ref[...] = jnp.concatenate(gates, axis=0)


def pack_a_kernel(top, rows, capacity, wanted_ref, *refs):
    parts, infos, outs = refs[:4], refs[4:8], refs[8:12]
    slot_ref, gate_ref, chosen = refs[12:]
    size = 8 * capacity

    @pl.when(pl.program_id(0) == 0)
    def _():
        info = jnp.concatenate([ref[...].astype(f32) for ref in infos], axis=0)
        slots_of(info, wanted_ref, top, rows, capacity, slot_ref, gate_ref)
        for d in range(4):
            chosen[d * size : (d + 1) * size, :] = jnp.where(
                one_hot(slot_ref, 0, d, size), 1.0, 0.0
            ).astype(bf16)

    values = jnp.concatenate([ref[...] for ref in parts], axis=0)
    for d in range(4):
        outs[d][...] = dot(chosen[d * size : (d + 1) * size, :], values).astype(bf16)


def pack_a(parts, wanted, top, rows, capacity, steps=2):
    pair, width = parts[0].shape
    width -= 128
    size, count = 8 * capacity, 4 * pair
    tile = width // steps
    fixed = pl.BlockSpec((8, count), lambda i: (0, 0))
    out = pl.pallas_call(
        functools.partial(pack_a_kernel, top, rows, capacity),
        grid=(steps,),
        in_specs=[SMEM]
        + [pl.BlockSpec((pair, tile), lambda i: (0, i))] * 4
        + [pl.BlockSpec((pair, 128), lambda i: (0, width // 128))] * 4,
        out_specs=[pl.BlockSpec((size, tile), lambda i: (0, i))] * 4 + [fixed] * 2,
        out_shape=[jax.ShapeDtypeStruct((size, width), bf16)] * 4
        + [jax.ShapeDtypeStruct((8, count), jnp.int32), jax.ShapeDtypeStruct((8, count), f32)],
        scratch_shapes=[pltpu.VMEM((4 * size, count), bf16)],
        compiler_params=ROOM,
        cost_estimate=LIGHT,
        name="pack_a",
    )(wanted, *parts, *parts)
    return out[:4], out[4], out[5]


def pack_b_kernel(size, scaled, slot_ref, gate_ref, *refs):
    parts, outs = refs[:5], refs[5:9]
    chosen, weight = refs[9:]

    @pl.when(pl.program_id(0) == 0)
    def _():
        for d in range(4):
            here = one_hot(slot_ref, 4, d, size)
            chosen[d * size : (d + 1) * size, :] = jnp.where(here, 1.0, 0.0).astype(bf16)
            weight[d * size : (d + 1) * size, :] = jnp.sum(
                jnp.where(here, gate_ref[4 + d : 5 + d, :], 0.0), axis=1, keepdims=True
            )

    values = jnp.concatenate([ref[...] for ref in parts], axis=0)
    for d in range(4):
        at = slice(d * size, (d + 1) * size)
        picked = dot(chosen[at, :], values)
        outs[d][...] = (picked * weight[at, :] if scaled else picked).astype(bf16)


def pack_b(parts, slot, gate, capacity, scaled, steps=2):
    pair, width = parts[0].shape
    width = width // 2
    size, count = 8 * capacity, 4 * pair
    tile = width // steps
    start = steps if scaled else 0
    fixed = pl.BlockSpec((8, count), lambda i: (0, 0))
    return pl.pallas_call(
        functools.partial(pack_b_kernel, size, scaled),
        grid=(steps,),
        in_specs=[fixed] * 2 + [
            pl.BlockSpec((part.shape[0], tile), lambda i: (0, start + i)) for part in parts
        ],
        out_specs=[pl.BlockSpec((size, tile), lambda i: (0, i))] * 4,
        out_shape=[jax.ShapeDtypeStruct((size, width), bf16)] * 4,
        scratch_shapes=[pltpu.VMEM((4 * size, count), bf16), pltpu.VMEM((4 * size, 1), f32)],
        compiler_params=ROOM,
        cost_estimate=LIGHT,
        name="pack_grads_b" if scaled else "pack_tokens_b",
    )(slot, gate, *parts)


def combine_kernel(first, size, pair, slot_ref, gate_ref, *refs):
    parts, own_ref, outs, weights = refs[:4], refs[4], refs[5:8], refs[8]

    @pl.when(pl.program_id(0) == 0)
    def _():
        for d in range(4):
            here = one_hot(slot_ref, first, d, size)
            scale = gate_ref[d : d + 1, :] if first == 0 else 1.0
            weights[d * size : (d + 1) * size, :] = jnp.where(here, scale, 0.0).astype(bf16)

    values = jnp.concatenate([ref[...] for ref in parts], axis=0)
    total = t_dot(weights[...], values)
    own_ref[...] = total[:pair]
    for d in range(3):
        outs[d][...] = total[(d + 1) * pair : (d + 2) * pair].astype(bf16)


def combine(chunks, slot, gate, first, steps=2):
    size, width = chunks[0].shape
    count = slot.shape[1]
    pair = count // 4
    tile = width // steps
    fixed = pl.BlockSpec((8, count), lambda i: (0, 0))
    block = pl.BlockSpec((pair, tile), lambda i: (0, i))
    return pl.pallas_call(
        functools.partial(combine_kernel, first, size, pair),
        grid=(steps,),
        in_specs=[fixed] * 2 + [pl.BlockSpec((size, tile), lambda i: (0, i))] * 4,
        out_specs=[block] * 4,
        out_shape=[jax.ShapeDtypeStruct((pair, width), f32)]
        + [jax.ShapeDtypeStruct((pair, width), bf16)] * 3,
        scratch_shapes=[pltpu.VMEM((4 * size, count), bf16)],
        compiler_params=ROOM,
        cost_estimate=LIGHT,
        name="combine_a" if first == 0 else "combine_b",
    )(slot, gate, *chunks)


def row_pair(rows):
    return jnp.concatenate([rows, send(rows, flip_row)], axis=0)


def spread(pair):
    far = send(pair, shift_near(2))
    up = send(pair, shift_near(1))
    down = send(pair, shift_near(3))
    return pair, up, far, down


def spread_in_steps(pair):
    rows = pair.shape[0] // 2
    up = send(pair, shift_near(1))
    down = send(pair, shift_near(3))
    first = send(down[:rows], shift_near(3))
    last = send(up[rows:], shift_near(1))
    return pair, up, first, last, down


def exchange(chunks, back=False):
    sign = -1 if back else 1
    two = send(chunks[2], shift_far(2))
    one = send(chunks[1], shift_far(sign % 4))
    three = send(chunks[3], shift_far(-sign % 4))
    return chunks[0], one, two, three


def gather_back(partials):
    own, one, two, three = partials
    two = send(two, shift_near(2))
    one = send(one, shift_near(3))
    three = send(three, shift_near(1))
    return own + one.astype(f32) + two.astype(f32) + three.astype(f32)


def finish(total, rows):
    other = send(total[rows:].astype(bf16), flip_row)
    return (total[:rows] + other.astype(f32)).astype(bf16)


def across(value, blocks=4):
    rows, cols = value.shape
    piece = rows // (blocks * blocks)
    cut = value.reshape(blocks, blocks, piece, cols)
    return jnp.swapaxes(cut, 0, 1).reshape(rows, cols)


def per_device(
    tokens_a, routes_a, gates_a, tokens_b, routes_b, gates_b, grad_b, w_gate, w_up, w_down
):
    rows, quarter = tokens_a.shape
    top_k = routes_a.shape[1]
    experts = GROUPS
    capacity = min(rows, 5 * rows * top_k // (4 * experts))
    half = w_gate.shape[2] // 2
    w_gate, w_up, w_down = w_gate[0], w_up[0], w_down[0]
    core = lax.axis_index("pipe") % 2
    mine = lax.axis_index("expert")
    step = jnp.arange(4, dtype=jnp.int32)
    along_x = mine - mine % 4 + (mine + step) % 4
    along_z = (mine + 8 * step) % 32
    wanted = jnp.where(core == 0, along_x, along_z)

    payload_a, payload_b = payload(
        tokens_a, tokens_b, grad_b, routes_a, gates_a, routes_b, gates_b
    )
    pair_a, pair_b = row_pair(payload_a), row_pair(payload_b)
    spread_a = spread(pair_a)
    size = 8 * capacity

    def chunks(value):
        return [value[d * size : (d + 1) * size] for d in range(4)]

    def given(parts):
        kept, gone = [], []
        for part in parts:
            low, top = part[:, :half], part[:, half:]
            kept.append(jnp.where(core == 0, low, top))
            gone.append(jnp.where(core == 0, top, low).astype(bf16))
        got = across(send(jnp.concatenate(gone, axis=1), flip_core))
        own = jnp.concatenate(kept, axis=1) + got.astype(f32)
        return own, own.astype(bf16)

    def halves(own, far):
        total = own + far.astype(f32)
        return [total[:, i : i + half] for i in range(0, total.shape[1], half)]

    def whole(parts):
        own = jnp.concatenate(parts, axis=1)
        got = across(send(own, flip_core))
        out = []
        for i in range(len(parts)):
            a, b = own[:, i * half : (i + 1) * half], got[:, i * half : (i + 1) * half]
            out.append(
                jnp.concatenate([jnp.where(core == 0, a, b), jnp.where(core == 0, b, a)], axis=1)
            )
        return out

    wanted = after(wanted, pair_b)
    packs_a, slot, gate = pack_a(spread_a, wanted, top_k, rows, capacity)
    recv_a = exchange(packs_a)
    spread_b = spread_in_steps(after(pair_b, slot))
    packs_b = pack_b(spread_b, slot, gate, capacity, False)
    packs_g = pack_b(spread_b, after(slot, packs_b), gate, capacity, True)

    xa = jnp.concatenate(after(recv_a, spread_b[1], spread_b[4]), axis=0)
    own_a, sent_a = given([dot(xa, w_gate), dot(xa, w_up)])
    far_a = send(sent_a, flip_chip)

    recv_b = exchange(after(packs_b, sent_a))
    recv_g = exchange(after(packs_g, sent_a))

    xb = jnp.concatenate(after(recv_b, far_a, recv_g[2]), axis=0)
    own_b, sent_b = given([dot(xb, w_gate), dot(xb, w_up)])
    far_b = send(sent_b, flip_chip)

    gate_a, up_a = halves(own_a, after(far_a, sent_b))
    (hidden_a,) = whole([(jax.nn.silu(gate_a) * up_a).astype(bf16)])
    out_a = dot(hidden_a, w_down).astype(bf16)
    back_a = exchange(chunks(out_a), back=True)

    gb = jnp.concatenate(after(recv_g, out_a), axis=0)
    own_h, sent_h = given([dot_t(gb, w_down)])
    far_h = send(sent_h, flip_chip)

    partial_a = combine(after(back_a, sent_h), slot, gate, 0)
    total_a = gather_back(partial_a)
    gate_b, up_b = halves(own_b, after(far_b, partial_a[1]))
    act = jax.nn.silu(gate_b)
    (dh,) = halves(own_h, after(far_h, total_a))
    hidden_b, d_gate, d_up = whole(
        [
            (act * up_b).astype(bf16),
            (dh * up_b * silu_slope(gate_b)).astype(bf16),
            (dh * act).astype(bf16),
        ]
    )
    dxb = (dot_t(d_gate, w_gate) + dot_t(d_up, w_up)).astype(bf16)
    back_b = exchange(chunks(dxb), back=True)
    mixed_a = finish(after(total_a, dxb), rows)
    grad_tokens_b = finish(gather_back(combine(back_b, slot, gate, 4)), rows)
    grad_gate = t_dot(xb, d_gate).astype(bf16)
    grad_up = t_dot(xb, d_up).astype(bf16)
    grad_down = t_dot(hidden_b, gb).astype(bf16)
    return (mixed_a, grad_tokens_b, grad_gate[None], grad_up[None], grad_down[None])


def solution(mesh):
    return jax.shard_map(
        per_device,
        mesh=mesh,
        in_specs=(
            P("expert", "pipe"),
            P("expert", None),
            P("expert", None),
            P("expert", "pipe"),
            P("expert", None),
            P("expert", None),
            P("expert", "pipe"),
            P("expert", "pipe", None),
            P("expert", "pipe", None),
            P("expert", None, "pipe"),
        ),
        out_specs=(
            P("expert", "pipe"),
            P("expert", "pipe"),
            P("expert", "pipe", None),
            P("expert", "pipe", None),
            P("expert", None, "pipe"),
        ),
        check_vma=False,
    )
```

```python
import functools

import jax
import jax.numpy as jnp
from jax import lax
from jax.experimental import pallas as pl
from jax.experimental.pallas import tpu as pltpu
from jax.sharding import PartitionSpec as P

BOTH = ("pipe", "expert")
PIPE = 4
GROUPS = 32
bf16 = jnp.bfloat16
f32 = jnp.float32


def after(value, *others):
    return lax.optimization_barrier((value, others))[0]


def split_place(pipe, expert):
    return pipe // 2, pipe % 2, expert // 8, (expert // 4) % 2, expert % 4


def moved(move):
    pairs = []
    for pipe in range(PIPE):
        for expert in range(GROUPS):
            yl, c, z, yh, x = move(*split_place(pipe, expert))
            target = (yl * 2 + c) * GROUPS + z * 8 + yh * 4 + x
            pairs.append((pipe * GROUPS + expert, target))
    return pairs


def send(value, move):
    return lax.ppermute(value, BOTH, moved(move))


def shift_near(d):
    def move(yl, c, z, yh, x):
        return (yl, c, (z + d) % 4, yh, x) if c == 0 else (yl, c, z, yh, (x + d) % 4)

    return move


def shift_far(d):
    def move(yl, c, z, yh, x):
        return (yl, c, z, yh, (x + d) % 4) if c == 0 else (yl, c, (z + d) % 4, yh, x)

    return move


def flip_row(yl, c, z, yh, x):
    return (yl, c, z, 1 - yh, x)


def flip_core(yl, c, z, yh, x):
    return (yl, 1 - c, z, yh, x)


def flip_chip(yl, c, z, yh, x):
    return (1 - yl, c, z, yh, x)


def dot(a, b):
    return jnp.dot(a, b, preferred_element_type=f32)


def dot_t(a, b):
    return lax.dot_general(a, b, (((1,), (1,)), ((), ())), preferred_element_type=f32)


def t_dot(a, b):
    return lax.dot_general(a, b, (((0,), (0,)), ((), ())), preferred_element_type=f32)


def silu_slope(values):
    sigma = jax.nn.sigmoid(values)
    return sigma * (1.0 + values * (1.0 - sigma))


LIGHT = pl.CostEstimate(flops=1000, bytes_accessed=1000, transcendentals=0)
ROOM = pltpu.CompilerParams(vmem_limit_bytes=16 * 1024 * 1024)
SMEM = pl.BlockSpec(memory_space=pltpu.SMEM)


def place(part, offset):
    top = part.shape[0]
    rows = lax.broadcasted_iota(jnp.int32, (top, 128), 0)
    cols = lax.broadcasted_iota(jnp.int32, (top, 128), 1)
    return t_dot(part.astype(bf16), jnp.where(cols == rows + offset, 1.0, 0.0).astype(bf16))


def payload_kernel(
    tokens_ref, tokens_b_ref, grad_b_ref, routes_a_ref, gates_a_ref, routes_b_ref, gates_b_ref,
    out_ref, out_b_ref,
):
    width = tokens_ref.shape[1]
    out_b_ref[:, :width] = tokens_b_ref[...]
    out_b_ref[:, width:] = grad_b_ref[...]
    out_ref[:, :width] = tokens_ref[...]
    info = None
    for i, (routes, gates) in enumerate(
        ((routes_a_ref, gates_a_ref), (routes_b_ref, gates_b_ref))
    ):
        top = gates.shape[0]
        high = gates[...].astype(bf16)
        low = gates[...] - high.astype(f32)
        for j, part in enumerate((routes[...].astype(f32), high, low)):
            placed = place(part, (3 * i + j) * top)
            info = placed if info is None else info + placed
    out_ref[:, width:] = info.astype(bf16)


def payload(tokens, tokens_b, grad_b, *tables):
    rows, width = tokens.shape
    return pl.pallas_call(
        payload_kernel,
        out_shape=[
            jax.ShapeDtypeStruct((rows, width + 128), bf16),
            jax.ShapeDtypeStruct((rows, 2 * width), bf16),
        ],
        cost_estimate=LIGHT,
        name="payload",
    )(tokens, tokens_b, grad_b, *[table.T for table in tables])


def one_hot(slot_ref, first, d, size):
    count = slot_ref.shape[1]
    index = lax.broadcasted_iota(jnp.int32, (size, count), 0)
    return slot_ref[first + d : first + d + 1, :] == index


def slots_of(info, wanted_ref, top, rows, capacity, slot_ref, gate_ref):
    count = info.shape[0]
    table = info.T
    hits, gates = [], []
    for i in range(2):
        base = 3 * i * top
        routes = table[base : base + top]
        gate = table[base + top : base + 2 * top] + table[base + 2 * top : base + 3 * top]
        for d in range(4):
            same = routes == wanted_ref[d].astype(f32)
            hits.append(jnp.sum(jnp.where(same, 1.0, 0.0), axis=0, keepdims=True))
            gates.append(jnp.sum(jnp.where(same, gate, 0.0), axis=0, keepdims=True))
    hit = jnp.concatenate(hits, axis=0)
    before = lax.broadcasted_iota(jnp.int32, (count, count), 0)
    token = lax.broadcasted_iota(jnp.int32, (count, count), 1)
    earlier = (before < token) & (before >= token - token % rows)
    position = dot(hit.astype(bf16), jnp.where(earlier, 1.0, 0.0).astype(bf16))
    block = lax.broadcasted_iota(jnp.int32, hit.shape, 1) // rows
    slot_ref[...] = jnp.where(hit > 0.0, block * capacity + position.astype(jnp.int32), -1)
    gate_ref[...] = jnp.concatenate(gates, axis=0)


def pack_a_kernel(top, rows, capacity, wanted_ref, *refs):
    parts, infos, outs = refs[:4], refs[4:8], refs[8:12]
    slot_ref, gate_ref, chosen = refs[12:]
    size = 8 * capacity

    @pl.when(pl.program_id(0) == 0)
    def _():
        info = jnp.concatenate([ref[...].astype(f32) for ref in infos], axis=0)
        slots_of(info, wanted_ref, top, rows, capacity, slot_ref, gate_ref)
        for d in range(4):
            chosen[d * size : (d + 1) * size, :] = jnp.where(
                one_hot(slot_ref, 0, d, size), 1.0, 0.0
            ).astype(bf16)

    values = jnp.concatenate([ref[...] for ref in parts], axis=0)
    for d in range(4):
        outs[d][...] = dot(chosen[d * size : (d + 1) * size, :], values).astype(bf16)


def pack_a(parts, wanted, top, rows, capacity, steps=2):
    pair, width = parts[0].shape
    width -= 128
    size, count = 8 * capacity, 4 * pair
    tile = width // steps
    fixed = pl.BlockSpec((8, count), lambda i: (0, 0))
    out = pl.pallas_call(
        functools.partial(pack_a_kernel, top, rows, capacity),
        grid=(steps,),
        in_specs=[SMEM]
        + [pl.BlockSpec((pair, tile), lambda i: (0, i))] * 4
        + [pl.BlockSpec((pair, 128), lambda i: (0, width // 128))] * 4,
        out_specs=[pl.BlockSpec((size, tile), lambda i: (0, i))] * 4 + [fixed] * 2,
        out_shape=[jax.ShapeDtypeStruct((size, width), bf16)] * 4
        + [jax.ShapeDtypeStruct((8, count), jnp.int32), jax.ShapeDtypeStruct((8, count), f32)],
        scratch_shapes=[pltpu.VMEM((4 * size, count), bf16)],
        compiler_params=ROOM,
        cost_estimate=LIGHT,
        name="pack_a",
    )(wanted, *parts, *parts)
    return out[:4], out[4], out[5]


def pack_b_kernel(size, half_steps, slot_ref, gate_ref, *refs):
    parts, outs = refs[:5], refs[5:9]
    chosen, weight = refs[9:]

    @pl.when(pl.program_id(0) == 0)
    def _():
        for d in range(4):
            here = one_hot(slot_ref, 4, d, size)
            chosen[d * size : (d + 1) * size, :] = jnp.where(here, 1.0, 0.0).astype(bf16)
            weight[d * size : (d + 1) * size, :] = jnp.sum(
                jnp.where(here, gate_ref[4 + d : 5 + d, :], 0.0), axis=1, keepdims=True
            )

    values = jnp.concatenate([ref[...] for ref in parts], axis=0)
    scaled = pl.program_id(0) >= half_steps
    for d in range(4):
        at = slice(d * size, (d + 1) * size)
        scale = jnp.where(scaled, weight[at, :], 1.0)
        outs[d][...] = (dot(chosen[at, :], values) * scale).astype(bf16)


def pack_b(parts, slot, gate, capacity, steps=4):
    pair, width = parts[0].shape
    size, count = 8 * capacity, 4 * pair
    tile = width // steps
    fixed = pl.BlockSpec((8, count), lambda i: (0, 0))
    return pl.pallas_call(
        functools.partial(pack_b_kernel, size, steps // 2),
        grid=(steps,),
        in_specs=[fixed] * 2 + [
            pl.BlockSpec((part.shape[0], tile), lambda i: (0, i)) for part in parts
        ],
        out_specs=[pl.BlockSpec((size, tile), lambda i: (0, i))] * 4,
        out_shape=[jax.ShapeDtypeStruct((size, width), bf16)] * 4,
        scratch_shapes=[pltpu.VMEM((4 * size, count), bf16), pltpu.VMEM((4 * size, 1), f32)],
        compiler_params=ROOM,
        cost_estimate=LIGHT,
        name="pack_b",
    )(slot, gate, *parts)


def combine_kernel(first, size, pair, slot_ref, gate_ref, *refs):
    parts, own_ref, outs, weights = refs[:4], refs[4], refs[5:8], refs[8]

    @pl.when(pl.program_id(0) == 0)
    def _():
        for d in range(4):
            here = one_hot(slot_ref, first, d, size)
            scale = gate_ref[d : d + 1, :] if first == 0 else 1.0
            weights[d * size : (d + 1) * size, :] = jnp.where(here, scale, 0.0).astype(bf16)

    values = jnp.concatenate([ref[...] for ref in parts], axis=0)
    total = t_dot(weights[...], values)
    own_ref[...] = total[:pair]
    for d in range(3):
        outs[d][...] = total[(d + 1) * pair : (d + 2) * pair].astype(bf16)


def combine(chunks, slot, gate, first, steps=2):
    size, width = chunks[0].shape
    count = slot.shape[1]
    pair = count // 4
    tile = width // steps
    fixed = pl.BlockSpec((8, count), lambda i: (0, 0))
    block = pl.BlockSpec((pair, tile), lambda i: (0, i))
    return pl.pallas_call(
        functools.partial(combine_kernel, first, size, pair),
        grid=(steps,),
        in_specs=[fixed] * 2 + [pl.BlockSpec((size, tile), lambda i: (0, i))] * 4,
        out_specs=[block] * 4,
        out_shape=[jax.ShapeDtypeStruct((pair, width), f32)]
        + [jax.ShapeDtypeStruct((pair, width), bf16)] * 3,
        scratch_shapes=[pltpu.VMEM((4 * size, count), bf16)],
        compiler_params=ROOM,
        cost_estimate=LIGHT,
        name="combine_a" if first == 0 else "combine_b",
    )(slot, gate, *chunks)


def row_pair(rows):
    return jnp.concatenate([rows, send(rows, flip_row)], axis=0)


def spread(pair):
    far = send(pair, shift_near(2))
    up = send(pair, shift_near(1))
    down = send(pair, shift_near(3))
    return pair, up, far, down


def spread_in_steps(pair):
    rows = pair.shape[0] // 2
    up = send(pair, shift_near(1))
    down = send(pair, shift_near(3))
    first = send(down[:rows], shift_near(3))
    last = send(up[rows:], shift_near(1))
    return pair, up, first, last, down


def exchange(chunks, back=False):
    sign = -1 if back else 1
    two = send(chunks[2], shift_far(2))
    one = send(chunks[1], shift_far(sign % 4))
    three = send(chunks[3], shift_far(-sign % 4))
    return chunks[0], one, two, three


def gather_back(partials):
    own, one, two, three = partials
    two = send(two, shift_near(2))
    one = send(one, shift_near(3))
    three = send(three, shift_near(1))
    return own + one.astype(f32) + two.astype(f32) + three.astype(f32)


def finish(total, rows):
    other = send(total[rows:].astype(bf16), flip_row)
    return (total[:rows] + other.astype(f32)).astype(bf16)


def across(value, blocks=4):
    rows, cols = value.shape
    piece = rows // (blocks * blocks)
    cut = value.reshape(blocks, blocks, piece, cols)
    return jnp.swapaxes(cut, 0, 1).reshape(rows, cols)


def per_device(
    tokens_a, routes_a, gates_a, tokens_b, routes_b, gates_b, grad_b, w_gate, w_up, w_down
):
    rows, quarter = tokens_a.shape
    top_k = routes_a.shape[1]
    experts = GROUPS
    capacity = min(rows, 5 * rows * top_k // (4 * experts))
    half = w_gate.shape[2] // 2
    w_gate, w_up, w_down = w_gate[0], w_up[0], w_down[0]
    core = lax.axis_index("pipe") % 2
    mine = lax.axis_index("expert")
    step = jnp.arange(4, dtype=jnp.int32)
    along_x = mine - mine % 4 + (mine + step) % 4
    along_z = (mine + 8 * step) % 32
    wanted = jnp.where(core == 0, along_x, along_z)

    payload_a, payload_b = payload(
        tokens_a, tokens_b, grad_b, routes_a, gates_a, routes_b, gates_b
    )
    pair_a, pair_b = row_pair(payload_a), row_pair(payload_b)
    spread_a = spread(pair_a)
    size = 8 * capacity

    def chunks(value):
        return [value[d * size : (d + 1) * size] for d in range(4)]

    def given(parts, *others):
        kept, gone = [], []
        for part in parts:
            low, top = part[:, :half], part[:, half:]
            kept.append(jnp.where(core == 0, low, top))
            gone.append(jnp.where(core == 0, top, low).astype(bf16))
        got = across(send(after(jnp.concatenate(gone, axis=1), *others), flip_core))
        own = jnp.concatenate(kept, axis=1) + got.astype(f32)
        return own, own.astype(bf16)

    def halves(own, far):
        total = own + far.astype(f32)
        return [total[:, i : i + half] for i in range(0, total.shape[1], half)]

    def whole(parts):
        own = jnp.concatenate(parts, axis=1)
        got = across(send(own, flip_core))
        out = []
        for i in range(len(parts)):
            a, b = own[:, i * half : (i + 1) * half], got[:, i * half : (i + 1) * half]
            out.append(
                jnp.concatenate([jnp.where(core == 0, a, b), jnp.where(core == 0, b, a)], axis=1)
            )
        return out

    wanted = after(wanted, pair_b)
    packs_a, slot, gate = pack_a(spread_a, wanted, top_k, rows, capacity)
    recv_a = exchange(packs_a)
    spread_b = spread_in_steps(after(pair_b, slot))
    packs_b = pack_b(spread_b, slot, gate, capacity)

    xa = jnp.concatenate(after(recv_a, spread_b[1], spread_b[4]), axis=0)
    own_a, sent_a = given([dot(xa, w_gate), dot(xa, w_up)], spread_b[2], spread_b[3])
    far_a = send(sent_a, flip_chip)

    recv_b = exchange(after(packs_b, sent_a))
    both_b = jnp.concatenate(after(recv_b, far_a), axis=0)
    xb, gb = both_b[:, :quarter], both_b[:, quarter:]
    own_b, sent_b = given([dot(xb, w_gate), dot(xb, w_up), dot_t(gb, w_down)])
    far_b = send(sent_b, flip_chip)

    gate_a, up_a = halves(own_a, after(far_a, sent_b))
    (hidden_a,) = whole([(jax.nn.silu(gate_a) * up_a).astype(bf16)])
    out_a = dot(hidden_a, w_down).astype(bf16)
    partial_a = combine(exchange(chunks(out_a), back=True), slot, gate, 0)

    total_a = gather_back(partial_a)
    gate_b, up_b, dh = halves(own_b, after(far_b, total_a))
    act = jax.nn.silu(gate_b)
    hidden_b, d_gate, d_up = whole(
        [
            (act * up_b).astype(bf16),
            (dh * up_b * silu_slope(gate_b)).astype(bf16),
            (dh * act).astype(bf16),
        ]
    )
    dxb = (dot_t(d_gate, w_gate) + dot_t(d_up, w_up)).astype(bf16)
    back_b = exchange(chunks(dxb), back=True)
    mixed_a = finish(after(total_a, dxb), rows)
    grad_tokens_b = finish(gather_back(combine(back_b, slot, gate, 4)), rows)
    grad_gate = t_dot(xb, d_gate).astype(bf16)
    grad_up = t_dot(xb, d_up).astype(bf16)
    grad_down = t_dot(hidden_b, gb).astype(bf16)
    return (mixed_a, grad_tokens_b, grad_gate[None], grad_up[None], grad_down[None])


def solution(mesh):
    return jax.shard_map(
        per_device,
        mesh=mesh,
        in_specs=(
            P("expert", "pipe"),
            P("expert", None),
            P("expert", None),
            P("expert", "pipe"),
            P("expert", None),
            P("expert", None),
            P("expert", "pipe"),
            P("expert", "pipe", None),
            P("expert", "pipe", None),
            P("expert", None, "pipe"),
        ),
        out_specs=(
            P("expert", "pipe"),
            P("expert", "pipe"),
            P("expert", "pipe", None),
            P("expert", "pipe", None),
            P("expert", None, "pipe"),
        ),
        check_vma=False,
    )
```

```python
import functools

import jax
import jax.numpy as jnp
from jax import lax
from jax.experimental import pallas as pl
from jax.experimental.pallas import tpu as pltpu
from jax.sharding import PartitionSpec as P

BOTH = ("pipe", "expert")
PIPE = 4
GROUPS = 32
bf16 = jnp.bfloat16
f32 = jnp.float32


def after(value, *others):
    return lax.optimization_barrier((value, others))[0]


def split_place(pipe, expert):
    return pipe // 2, pipe % 2, expert // 8, (expert // 4) % 2, expert % 4


def moved(move):
    pairs = []
    for pipe in range(PIPE):
        for expert in range(GROUPS):
            yl, c, z, yh, x = move(*split_place(pipe, expert))
            target = (yl * 2 + c) * GROUPS + z * 8 + yh * 4 + x
            pairs.append((pipe * GROUPS + expert, target))
    return pairs


def send(value, move):
    return lax.ppermute(value, BOTH, moved(move))


def shift_near(d):
    def move(yl, c, z, yh, x):
        return (yl, c, (z + d) % 4, yh, x) if c == 0 else (yl, c, z, yh, (x + d) % 4)

    return move


def shift_far(d):
    def move(yl, c, z, yh, x):
        return (yl, c, z, yh, (x + d) % 4) if c == 0 else (yl, c, (z + d) % 4, yh, x)

    return move


def flip_row(yl, c, z, yh, x):
    return (yl, c, z, 1 - yh, x)


def flip_core(yl, c, z, yh, x):
    return (yl, 1 - c, z, yh, x)


def flip_chip(yl, c, z, yh, x):
    return (1 - yl, c, z, yh, x)


def dot(a, b):
    return jnp.dot(a, b, preferred_element_type=f32)


def dot_t(a, b):
    return lax.dot_general(a, b, (((1,), (1,)), ((), ())), preferred_element_type=f32)


def t_dot(a, b):
    return lax.dot_general(a, b, (((0,), (0,)), ((), ())), preferred_element_type=f32)


def silu_slope(values):
    sigma = jax.nn.sigmoid(values)
    return sigma * (1.0 + values * (1.0 - sigma))


LIGHT = pl.CostEstimate(flops=1000, bytes_accessed=1000, transcendentals=0)
ROOM = pltpu.CompilerParams(vmem_limit_bytes=16 * 1024 * 1024)
SMEM = pl.BlockSpec(memory_space=pltpu.SMEM)


def place(part, offset):
    top = part.shape[0]
    rows = lax.broadcasted_iota(jnp.int32, (top, 128), 0)
    cols = lax.broadcasted_iota(jnp.int32, (top, 128), 1)
    return t_dot(part.astype(bf16), jnp.where(cols == rows + offset, 1.0, 0.0).astype(bf16))


def payload_kernel(
    tokens_ref, tokens_b_ref, grad_b_ref, routes_a_ref, gates_a_ref, routes_b_ref, gates_b_ref,
    out_ref, out_b_ref,
):
    width = tokens_ref.shape[1]
    out_b_ref[:, :width] = tokens_b_ref[...]
    out_b_ref[:, width:] = grad_b_ref[...]
    out_ref[:, :width] = tokens_ref[...]
    info = None
    for i, (routes, gates) in enumerate(
        ((routes_a_ref, gates_a_ref), (routes_b_ref, gates_b_ref))
    ):
        top = gates.shape[0]
        high = gates[...].astype(bf16)
        low = gates[...] - high.astype(f32)
        for j, part in enumerate((routes[...].astype(f32), high, low)):
            placed = place(part, (3 * i + j) * top)
            info = placed if info is None else info + placed
    out_ref[:, width:] = info.astype(bf16)


def payload(tokens, tokens_b, grad_b, *tables):
    rows, width = tokens.shape
    return pl.pallas_call(
        payload_kernel,
        out_shape=[
            jax.ShapeDtypeStruct((rows, width + 128), bf16),
            jax.ShapeDtypeStruct((rows, 2 * width), bf16),
        ],
        cost_estimate=LIGHT,
        name="payload",
    )(tokens, tokens_b, grad_b, *[table.T for table in tables])


def one_hot(slot_ref, first, d, size):
    count = slot_ref.shape[1]
    index = lax.broadcasted_iota(jnp.int32, (size, count), 0)
    return slot_ref[first + d : first + d + 1, :] == index


def slots_of(info, wanted_ref, top, rows, capacity, slot_ref, gate_ref):
    count = info.shape[0]
    table = info.T
    hits, gates = [], []
    for i in range(2):
        base = 3 * i * top
        routes = table[base : base + top]
        gate = table[base + top : base + 2 * top] + table[base + 2 * top : base + 3 * top]
        for d in range(4):
            same = routes == wanted_ref[d].astype(f32)
            hits.append(jnp.sum(jnp.where(same, 1.0, 0.0), axis=0, keepdims=True))
            gates.append(jnp.sum(jnp.where(same, gate, 0.0), axis=0, keepdims=True))
    hit = jnp.concatenate(hits, axis=0)
    before = lax.broadcasted_iota(jnp.int32, (count, count), 0)
    token = lax.broadcasted_iota(jnp.int32, (count, count), 1)
    earlier = (before < token) & (before >= token - token % rows)
    position = dot(hit.astype(bf16), jnp.where(earlier, 1.0, 0.0).astype(bf16))
    block = lax.broadcasted_iota(jnp.int32, hit.shape, 1) // rows
    slot_ref[...] = jnp.where(hit > 0.0, block * capacity + position.astype(jnp.int32), -1)
    gate_ref[...] = jnp.concatenate(gates, axis=0)


def pack_a_kernel(top, rows, capacity, wanted_ref, *refs):
    parts, infos, outs = refs[:4], refs[4:8], refs[8:12]
    slot_ref, gate_ref, chosen = refs[12:]
    size = 8 * capacity

    @pl.when(pl.program_id(0) == 0)
    def _():
        info = jnp.concatenate([ref[...].astype(f32) for ref in infos], axis=0)
        slots_of(info, wanted_ref, top, rows, capacity, slot_ref, gate_ref)
        for d in range(4):
            chosen[d * size : (d + 1) * size, :] = jnp.where(
                one_hot(slot_ref, 0, d, size), 1.0, 0.0
            ).astype(bf16)

    values = jnp.concatenate([ref[...] for ref in parts], axis=0)
    for d in range(4):
        outs[d][...] = dot(chosen[d * size : (d + 1) * size, :], values).astype(bf16)


def pack_a(parts, wanted, top, rows, capacity, steps=2):
    pair, width = parts[0].shape
    width -= 128
    size, count = 8 * capacity, 4 * pair
    tile = width // steps
    fixed = pl.BlockSpec((8, count), lambda i: (0, 0))
    out = pl.pallas_call(
        functools.partial(pack_a_kernel, top, rows, capacity),
        grid=(steps,),
        in_specs=[SMEM]
        + [pl.BlockSpec((pair, tile), lambda i: (0, i))] * 4
        + [pl.BlockSpec((pair, 128), lambda i: (0, width // 128))] * 4,
        out_specs=[pl.BlockSpec((size, tile), lambda i: (0, i))] * 4 + [fixed] * 2,
        out_shape=[jax.ShapeDtypeStruct((size, width), bf16)] * 4
        + [jax.ShapeDtypeStruct((8, count), jnp.int32), jax.ShapeDtypeStruct((8, count), f32)],
        scratch_shapes=[pltpu.VMEM((4 * size, count), bf16)],
        compiler_params=ROOM,
        cost_estimate=LIGHT,
        name="pack_a",
    )(wanted, *parts, *parts)
    return out[:4], out[4], out[5]


def pack_b_kernel(size, half_steps, slot_ref, gate_ref, *refs):
    parts, outs = refs[:5], refs[5:9]
    chosen, weight = refs[9:]

    @pl.when(pl.program_id(0) == 0)
    def _():
        for d in range(4):
            here = one_hot(slot_ref, 4, d, size)
            chosen[d * size : (d + 1) * size, :] = jnp.where(here, 1.0, 0.0).astype(bf16)
            weight[d * size : (d + 1) * size, :] = jnp.sum(
                jnp.where(here, gate_ref[4 + d : 5 + d, :], 0.0), axis=1, keepdims=True
            )

    values = jnp.concatenate([ref[...] for ref in parts], axis=0)
    scaled = pl.program_id(0) >= half_steps
    for d in range(4):
        at = slice(d * size, (d + 1) * size)
        scale = jnp.where(scaled, weight[at, :], 1.0)
        outs[d][...] = (dot(chosen[at, :], values) * scale).astype(bf16)


def pack_b(parts, slot, gate, capacity, steps=4):
    pair, width = parts[0].shape
    size, count = 8 * capacity, 4 * pair
    tile = width // steps
    fixed = pl.BlockSpec((8, count), lambda i: (0, 0))
    return pl.pallas_call(
        functools.partial(pack_b_kernel, size, steps // 2),
        grid=(steps,),
        in_specs=[fixed] * 2 + [
            pl.BlockSpec((part.shape[0], tile), lambda i: (0, i)) for part in parts
        ],
        out_specs=[pl.BlockSpec((size, tile), lambda i: (0, i))] * 4,
        out_shape=[jax.ShapeDtypeStruct((size, width), bf16)] * 4,
        scratch_shapes=[pltpu.VMEM((4 * size, count), bf16), pltpu.VMEM((4 * size, 1), f32)],
        compiler_params=ROOM,
        cost_estimate=LIGHT,
        name="pack_b",
    )(slot, gate, *parts)


def combine_kernel(first, size, pair, slot_ref, gate_ref, *refs):
    parts, own_ref, outs, weights = refs[:4], refs[4], refs[5:8], refs[8]

    @pl.when(pl.program_id(0) == 0)
    def _():
        for d in range(4):
            here = one_hot(slot_ref, first, d, size)
            scale = gate_ref[d : d + 1, :] if first == 0 else 1.0
            weights[d * size : (d + 1) * size, :] = jnp.where(here, scale, 0.0).astype(bf16)

    values = jnp.concatenate([ref[...] for ref in parts], axis=0)
    total = t_dot(weights[...], values)
    own_ref[...] = total[:pair]
    for d in range(3):
        outs[d][...] = total[(d + 1) * pair : (d + 2) * pair].astype(bf16)


def combine(chunks, slot, gate, first, steps=2):
    size, width = chunks[0].shape
    count = slot.shape[1]
    pair = count // 4
    tile = width // steps
    fixed = pl.BlockSpec((8, count), lambda i: (0, 0))
    block = pl.BlockSpec((pair, tile), lambda i: (0, i))
    return pl.pallas_call(
        functools.partial(combine_kernel, first, size, pair),
        grid=(steps,),
        in_specs=[fixed] * 2 + [pl.BlockSpec((size, tile), lambda i: (0, i))] * 4,
        out_specs=[block] * 4,
        out_shape=[jax.ShapeDtypeStruct((pair, width), f32)]
        + [jax.ShapeDtypeStruct((pair, width), bf16)] * 3,
        scratch_shapes=[pltpu.VMEM((4 * size, count), bf16)],
        compiler_params=ROOM,
        cost_estimate=LIGHT,
        name="combine_a" if first == 0 else "combine_b",
    )(slot, gate, *chunks)


def row_pair(rows):
    return jnp.concatenate([rows, send(rows, flip_row)], axis=0)


def spread(pair):
    far = send(pair, shift_near(2))
    up = send(pair, shift_near(1))
    down = send(pair, shift_near(3))
    return pair, up, far, down


def spread_in_steps(pair):
    rows = pair.shape[0] // 2
    up = send(pair, shift_near(1))
    down = send(pair, shift_near(3))
    first = send(down[:rows], shift_near(3))
    last = send(up[rows:], shift_near(1))
    return pair, up, first, last, down


def exchange(chunks, back=False):
    sign = -1 if back else 1
    two = send(chunks[2], shift_far(2))
    one = send(chunks[1], shift_far(sign % 4))
    three = send(chunks[3], shift_far(-sign % 4))
    return chunks[0], one, two, three


def gather_back(partials):
    own, one, two, three = partials
    two = send(two, shift_near(2))
    one = send(one, shift_near(3))
    three = send(three, shift_near(1))
    return own + one.astype(f32) + two.astype(f32) + three.astype(f32)


def finish(total, rows):
    other = send(total[rows:].astype(bf16), flip_row)
    return (total[:rows] + other.astype(f32)).astype(bf16)


def across(value, blocks=4):
    rows, cols = value.shape
    piece = rows // (blocks * blocks)
    cut = value.reshape(blocks, blocks, piece, cols)
    return jnp.swapaxes(cut, 0, 1).reshape(rows, cols)


def per_device(
    tokens_a, routes_a, gates_a, tokens_b, routes_b, gates_b, grad_b, w_gate, w_up, w_down
):
    rows, quarter = tokens_a.shape
    top_k = routes_a.shape[1]
    experts = GROUPS
    capacity = min(rows, 5 * rows * top_k // (4 * experts))
    half = w_gate.shape[2] // 2
    w_gate, w_up, w_down = w_gate[0], w_up[0], w_down[0]
    core = lax.axis_index("pipe") % 2
    mine = lax.axis_index("expert")
    step = jnp.arange(4, dtype=jnp.int32)
    along_x = mine - mine % 4 + (mine + step) % 4
    along_z = (mine + 8 * step) % 32
    wanted = jnp.where(core == 0, along_x, along_z)

    payload_a, payload_b = payload(
        tokens_a, tokens_b, grad_b, routes_a, gates_a, routes_b, gates_b
    )
    pair_a, pair_b = row_pair(payload_a), row_pair(payload_b)
    spread_a = spread(pair_a)
    size = 8 * capacity

    def chunks(value):
        return [value[d * size : (d + 1) * size] for d in range(4)]

    def given(parts, others=(), inside=()):
        kept, gone = [], []
        for part in parts:
            low, top = part[:, :half], part[:, half:]
            kept.append(jnp.where(core == 0, low, top))
            gone.append(jnp.where(core == 0, top, low).astype(bf16))
        got = send(after(jnp.concatenate(gone, axis=1), *others), flip_core)
        got = across(after(got, *inside))
        own = jnp.concatenate(kept, axis=1) + got.astype(f32)
        return own, own.astype(bf16)

    def halves(own, far):
        total = own + far.astype(f32)
        return [total[:, i : i + half] for i in range(0, total.shape[1], half)]

    def whole(parts):
        own = jnp.concatenate(parts, axis=1)
        got = across(send(own, flip_core))
        out = []
        for i in range(len(parts)):
            a, b = own[:, i * half : (i + 1) * half], got[:, i * half : (i + 1) * half]
            out.append(
                jnp.concatenate([jnp.where(core == 0, a, b), jnp.where(core == 0, b, a)], axis=1)
            )
        return out

    wanted = after(wanted, pair_b)
    packs_a, slot, gate = pack_a(spread_a, wanted, top_k, rows, capacity)
    recv_a = exchange(packs_a)
    spread_b = spread_in_steps(after(pair_b, slot))
    packs_b = pack_b(spread_b, slot, gate, capacity)

    xa = jnp.concatenate(after(recv_a, spread_b[1], spread_b[4]), axis=0)
    own_a, sent_a = given(
        [dot(xa, w_gate), dot(xa, w_up)], others=spread_b[2:4], inside=packs_b
    )
    far_a = send(sent_a, flip_chip)

    recv_b = exchange(after(packs_b, sent_a))
    both_b = jnp.concatenate(after(recv_b, far_a), axis=0)
    xb, gb = both_b[:, :quarter], both_b[:, quarter:]
    own_b, sent_b = given([dot(xb, w_gate), dot(xb, w_up), dot_t(gb, w_down)])
    far_b = send(sent_b, flip_chip)

    gate_a, up_a = halves(own_a, after(far_a, sent_b))
    (hidden_a,) = whole([(jax.nn.silu(gate_a) * up_a).astype(bf16)])
    out_a = dot(hidden_a, w_down).astype(bf16)
    partial_a = combine(exchange(chunks(out_a), back=True), slot, gate, 0)

    total_a = gather_back(partial_a)
    gate_b, up_b, dh = halves(own_b, after(far_b, total_a))
    act = jax.nn.silu(gate_b)
    hidden_b, d_gate, d_up = whole(
        [
            (act * up_b).astype(bf16),
            (dh * up_b * silu_slope(gate_b)).astype(bf16),
            (dh * act).astype(bf16),
        ]
    )
    dxb = (dot_t(d_gate, w_gate) + dot_t(d_up, w_up)).astype(bf16)
    back_b = exchange(chunks(dxb), back=True)
    mixed_a = finish(after(total_a, dxb), rows)
    grad_tokens_b = finish(gather_back(combine(back_b, slot, gate, 4)), rows)
    grad_gate = t_dot(xb, d_gate).astype(bf16)
    grad_up = t_dot(xb, d_up).astype(bf16)
    grad_down = t_dot(hidden_b, gb).astype(bf16)
    return (mixed_a, grad_tokens_b, grad_gate[None], grad_up[None], grad_down[None])


def solution(mesh):
    return jax.shard_map(
        per_device,
        mesh=mesh,
        in_specs=(
            P("expert", "pipe"),
            P("expert", None),
            P("expert", None),
            P("expert", "pipe"),
            P("expert", None),
            P("expert", None),
            P("expert", "pipe"),
            P("expert", "pipe", None),
            P("expert", "pipe", None),
            P("expert", None, "pipe"),
        ),
        out_specs=(
            P("expert", "pipe"),
            P("expert", "pipe"),
            P("expert", "pipe", None),
            P("expert", "pipe", None),
            P("expert", None, "pipe"),
        ),
        check_vma=False,
    )
```

```python
import functools

import jax
import jax.numpy as jnp
from jax import lax
from jax.experimental import pallas as pl
from jax.experimental.pallas import tpu as pltpu
from jax.sharding import PartitionSpec as P

BOTH = ("pipe", "expert")
PIPE = 4
GROUPS = 32
bf16 = jnp.bfloat16
f32 = jnp.float32


def after(value, *others):
    return lax.optimization_barrier((value, others))[0]


def split_place(pipe, expert):
    return pipe // 2, pipe % 2, expert // 8, (expert // 4) % 2, expert % 4


def moved(move):
    pairs = []
    for pipe in range(PIPE):
        for expert in range(GROUPS):
            yl, c, z, yh, x = move(*split_place(pipe, expert))
            target = (yl * 2 + c) * GROUPS + z * 8 + yh * 4 + x
            pairs.append((pipe * GROUPS + expert, target))
    return pairs


def send(value, move):
    return lax.ppermute(value, BOTH, moved(move))


def shift_near(d):
    def move(yl, c, z, yh, x):
        return (yl, c, (z + d) % 4, yh, x) if c == 0 else (yl, c, z, yh, (x + d) % 4)

    return move


def shift_far(d):
    def move(yl, c, z, yh, x):
        return (yl, c, z, yh, (x + d) % 4) if c == 0 else (yl, c, (z + d) % 4, yh, x)

    return move


def flip_row(yl, c, z, yh, x):
    return (yl, c, z, 1 - yh, x)


def flip_core(yl, c, z, yh, x):
    return (yl, 1 - c, z, yh, x)


def flip_chip(yl, c, z, yh, x):
    return (1 - yl, c, z, yh, x)


def dot(a, b):
    return jnp.dot(a, b, preferred_element_type=f32)


def dot_t(a, b):
    return lax.dot_general(a, b, (((1,), (1,)), ((), ())), preferred_element_type=f32)


def t_dot(a, b):
    return lax.dot_general(a, b, (((0,), (0,)), ((), ())), preferred_element_type=f32)


def silu_slope(values):
    sigma = jax.nn.sigmoid(values)
    return sigma * (1.0 + values * (1.0 - sigma))


LIGHT = pl.CostEstimate(flops=1000, bytes_accessed=1000, transcendentals=0)
ROOM = pltpu.CompilerParams(vmem_limit_bytes=16 * 1024 * 1024)
SMEM = pl.BlockSpec(memory_space=pltpu.SMEM)


def place(part, offset):
    top = part.shape[0]
    rows = lax.broadcasted_iota(jnp.int32, (top, 128), 0)
    cols = lax.broadcasted_iota(jnp.int32, (top, 128), 1)
    return t_dot(part.astype(bf16), jnp.where(cols == rows + offset, 1.0, 0.0).astype(bf16))


def payload_kernel(
    tokens_ref, tokens_b_ref, grad_b_ref, routes_a_ref, gates_a_ref, routes_b_ref, gates_b_ref,
    out_ref, out_b_ref,
):
    width = tokens_ref.shape[1]
    out_b_ref[:, :width] = tokens_b_ref[...]
    out_b_ref[:, width:] = grad_b_ref[...]
    out_ref[:, :width] = tokens_ref[...]
    info = None
    for i, (routes, gates) in enumerate(
        ((routes_a_ref, gates_a_ref), (routes_b_ref, gates_b_ref))
    ):
        top = gates.shape[0]
        high = gates[...].astype(bf16)
        low = gates[...] - high.astype(f32)
        for j, part in enumerate((routes[...].astype(f32), high, low)):
            placed = place(part, (3 * i + j) * top)
            info = placed if info is None else info + placed
    out_ref[:, width:] = info.astype(bf16)


def payload(tokens, tokens_b, grad_b, *tables):
    rows, width = tokens.shape
    return pl.pallas_call(
        payload_kernel,
        out_shape=[
            jax.ShapeDtypeStruct((rows, width + 128), bf16),
            jax.ShapeDtypeStruct((rows, 2 * width), bf16),
        ],
        cost_estimate=LIGHT,
        name="payload",
    )(tokens, tokens_b, grad_b, *[table.T for table in tables])


def one_hot(slot_ref, first, d, size):
    count = slot_ref.shape[1]
    index = lax.broadcasted_iota(jnp.int32, (size, count), 0)
    return slot_ref[first + d : first + d + 1, :] == index


def slots_of(info, wanted_ref, top, rows, capacity, slot_ref, gate_ref):
    count = info.shape[0]
    table = info.T
    hits, gates = [], []
    for i in range(2):
        base = 3 * i * top
        routes = table[base : base + top]
        gate = table[base + top : base + 2 * top] + table[base + 2 * top : base + 3 * top]
        for d in range(4):
            same = routes == wanted_ref[d].astype(f32)
            hits.append(jnp.sum(jnp.where(same, 1.0, 0.0), axis=0, keepdims=True))
            gates.append(jnp.sum(jnp.where(same, gate, 0.0), axis=0, keepdims=True))
    hit = jnp.concatenate(hits, axis=0)
    before = lax.broadcasted_iota(jnp.int32, (count, count), 0)
    token = lax.broadcasted_iota(jnp.int32, (count, count), 1)
    earlier = (before < token) & (before >= token - token % rows)
    position = dot(hit.astype(bf16), jnp.where(earlier, 1.0, 0.0).astype(bf16))
    block = lax.broadcasted_iota(jnp.int32, hit.shape, 1) // rows
    slot_ref[...] = jnp.where(hit > 0.0, block * capacity + position.astype(jnp.int32), -1)
    gate_ref[...] = jnp.concatenate(gates, axis=0)


def pack_a_kernel(top, rows, capacity, wanted_ref, *refs):
    parts, infos, outs = refs[:4], refs[4:8], refs[8:12]
    slot_ref, gate_ref, chosen = refs[12:]
    size = 8 * capacity

    @pl.when(pl.program_id(0) == 0)
    def _():
        info = jnp.concatenate([ref[...].astype(f32) for ref in infos], axis=0)
        slots_of(info, wanted_ref, top, rows, capacity, slot_ref, gate_ref)
        for d in range(4):
            chosen[d * size : (d + 1) * size, :] = jnp.where(
                one_hot(slot_ref, 0, d, size), 1.0, 0.0
            ).astype(bf16)

    values = jnp.concatenate([ref[...] for ref in parts], axis=0)
    for d in range(4):
        outs[d][...] = dot(chosen[d * size : (d + 1) * size, :], values).astype(bf16)


def pack_a(parts, wanted, top, rows, capacity, steps=2):
    pair, width = parts[0].shape
    width -= 128
    size, count = 8 * capacity, 4 * pair
    tile = width // steps
    fixed = pl.BlockSpec((8, count), lambda i: (0, 0))
    out = pl.pallas_call(
        functools.partial(pack_a_kernel, top, rows, capacity),
        grid=(steps,),
        in_specs=[SMEM]
        + [pl.BlockSpec((pair, tile), lambda i: (0, i))] * 4
        + [pl.BlockSpec((pair, 128), lambda i: (0, width // 128))] * 4,
        out_specs=[pl.BlockSpec((size, tile), lambda i: (0, i))] * 4 + [fixed] * 2,
        out_shape=[jax.ShapeDtypeStruct((size, width), bf16)] * 4
        + [jax.ShapeDtypeStruct((8, count), jnp.int32), jax.ShapeDtypeStruct((8, count), f32)],
        scratch_shapes=[pltpu.VMEM((4 * size, count), bf16)],
        compiler_params=ROOM,
        cost_estimate=LIGHT,
        name="pack_a",
    )(wanted, *parts, *parts)
    return out[:4], out[4], out[5]


def pack_b_kernel(size, half_steps, slot_ref, gate_ref, *refs):
    parts, outs = refs[:5], refs[5:9]
    chosen, weight = refs[9:]

    @pl.when(pl.program_id(0) == 0)
    def _():
        for d in range(4):
            here = one_hot(slot_ref, 4, d, size)
            chosen[d * size : (d + 1) * size, :] = jnp.where(here, 1.0, 0.0).astype(bf16)
            weight[d * size : (d + 1) * size, :] = jnp.sum(
                jnp.where(here, gate_ref[4 + d : 5 + d, :], 0.0), axis=1, keepdims=True
            )

    values = jnp.concatenate([ref[...] for ref in parts], axis=0)
    scaled = pl.program_id(0) >= half_steps
    for d in range(4):
        at = slice(d * size, (d + 1) * size)
        scale = jnp.where(scaled, weight[at, :], 1.0)
        outs[d][...] = (dot(chosen[at, :], values) * scale).astype(bf16)


def pack_b(parts, slot, gate, capacity, steps=4):
    pair, width = parts[0].shape
    size, count = 8 * capacity, 4 * pair
    tile = width // steps
    fixed = pl.BlockSpec((8, count), lambda i: (0, 0))
    return pl.pallas_call(
        functools.partial(pack_b_kernel, size, steps // 2),
        grid=(steps,),
        in_specs=[fixed] * 2 + [
            pl.BlockSpec((part.shape[0], tile), lambda i: (0, i)) for part in parts
        ],
        out_specs=[pl.BlockSpec((size, tile), lambda i: (0, i))] * 4,
        out_shape=[jax.ShapeDtypeStruct((size, width), bf16)] * 4,
        scratch_shapes=[pltpu.VMEM((4 * size, count), bf16), pltpu.VMEM((4 * size, 1), f32)],
        compiler_params=ROOM,
        cost_estimate=LIGHT,
        name="pack_b",
    )(slot, gate, *parts)


def combine_kernel(first, size, pair, slot_ref, gate_ref, *refs):
    parts, own_ref, outs, weights = refs[:4], refs[4], refs[5:8], refs[8]

    @pl.when(pl.program_id(0) == 0)
    def _():
        for d in range(4):
            here = one_hot(slot_ref, first, d, size)
            scale = gate_ref[d : d + 1, :] if first == 0 else 1.0
            weights[d * size : (d + 1) * size, :] = jnp.where(here, scale, 0.0).astype(bf16)

    values = jnp.concatenate([ref[...] for ref in parts], axis=0)
    total = t_dot(weights[...], values)
    own_ref[...] = total[:pair]
    for d in range(3):
        outs[d][...] = total[(d + 1) * pair : (d + 2) * pair].astype(bf16)


def combine(chunks, slot, gate, first, steps=2):
    size, width = chunks[0].shape
    count = slot.shape[1]
    pair = count // 4
    tile = width // steps
    fixed = pl.BlockSpec((8, count), lambda i: (0, 0))
    block = pl.BlockSpec((pair, tile), lambda i: (0, i))
    return pl.pallas_call(
        functools.partial(combine_kernel, first, size, pair),
        grid=(steps,),
        in_specs=[fixed] * 2 + [pl.BlockSpec((size, tile), lambda i: (0, i))] * 4,
        out_specs=[block] * 4,
        out_shape=[jax.ShapeDtypeStruct((pair, width), f32)]
        + [jax.ShapeDtypeStruct((pair, width), bf16)] * 3,
        scratch_shapes=[pltpu.VMEM((4 * size, count), bf16)],
        compiler_params=ROOM,
        cost_estimate=LIGHT,
        name="combine_a" if first == 0 else "combine_b",
    )(slot, gate, *chunks)


def row_pair(rows):
    return jnp.concatenate([rows, send(rows, flip_row)], axis=0)


def spread(pair):
    far = send(pair, shift_near(2))
    up = send(pair, shift_near(1))
    down = send(pair, shift_near(3))
    return pair, up, far, down


def spread_in_steps(pair):
    rows = pair.shape[0] // 2
    up = send(pair, shift_near(1))
    down = send(pair, shift_near(3))
    first = send(down[:rows], shift_near(3))
    last = send(up[rows:], shift_near(1))
    return pair, up, first, last, down


def exchange(chunks, back=False):
    sign = -1 if back else 1
    two = send(chunks[2], shift_far(2))
    one = send(chunks[1], shift_far(sign % 4))
    three = send(chunks[3], shift_far(-sign % 4))
    return chunks[0], one, two, three


def gather_back(partials):
    own, one, two, three = partials
    two = send(two, shift_near(2))
    one = send(one, shift_near(3))
    three = send(three, shift_near(1))
    return own + one.astype(f32) + two.astype(f32) + three.astype(f32)


def finish(total, rows):
    other = send(total[rows:].astype(bf16), flip_row)
    return (total[:rows] + other.astype(f32)).astype(bf16)


def across(value, blocks=4):
    rows, cols = value.shape
    piece = rows // (blocks * blocks)
    cut = value.reshape(blocks, blocks, piece, cols)
    return jnp.swapaxes(cut, 0, 1).reshape(rows, cols)


def per_device(
    tokens_a, routes_a, gates_a, tokens_b, routes_b, gates_b, grad_b, w_gate, w_up, w_down
):
    rows, quarter = tokens_a.shape
    top_k = routes_a.shape[1]
    experts = GROUPS
    capacity = min(rows, 5 * rows * top_k // (4 * experts))
    half = w_gate.shape[2] // 2
    w_gate, w_up, w_down = w_gate[0], w_up[0], w_down[0]
    core = lax.axis_index("pipe") % 2
    mine = lax.axis_index("expert")
    step = jnp.arange(4, dtype=jnp.int32)
    along_x = mine - mine % 4 + (mine + step) % 4
    along_z = (mine + 8 * step) % 32
    wanted = jnp.where(core == 0, along_x, along_z)

    payload_a, payload_b = payload(
        tokens_a, tokens_b, grad_b, routes_a, gates_a, routes_b, gates_b
    )
    pair_a, pair_b = row_pair(payload_a), row_pair(payload_b)
    spread_a = spread(pair_a)
    size = 8 * capacity

    def chunks(value):
        return [value[d * size : (d + 1) * size] for d in range(4)]

    def given(parts, others=(), inside=()):
        kept, gone = [], []
        for part in parts:
            low, top = part[:, :half], part[:, half:]
            kept.append(jnp.where(core == 0, low, top))
            gone.append(jnp.where(core == 0, top, low).astype(bf16))
        pieces = [
            after(jnp.concatenate(group, axis=1), *others) for group in (gone[:2], gone[2:]) if group
        ]
        got = jnp.concatenate(
            [across(after(send(piece, flip_core), *inside)) for piece in pieces], axis=1
        )
        own = jnp.concatenate(kept, axis=1) + got.astype(f32)
        return own, own.astype(bf16)

    def halves(own, far):
        total = own + far.astype(f32)
        return [total[:, i : i + half] for i in range(0, total.shape[1], half)]

    def whole(parts):
        own = jnp.concatenate(parts, axis=1)
        got = across(send(own, flip_core))
        out = []
        for i in range(len(parts)):
            a, b = own[:, i * half : (i + 1) * half], got[:, i * half : (i + 1) * half]
            out.append(
                jnp.concatenate([jnp.where(core == 0, a, b), jnp.where(core == 0, b, a)], axis=1)
            )
        return out

    wanted = after(wanted, pair_b)
    packs_a, slot, gate = pack_a(spread_a, wanted, top_k, rows, capacity)
    recv_a = exchange(packs_a)
    spread_b = spread_in_steps(after(pair_b, slot))
    packs_b = pack_b(spread_b, slot, gate, capacity)

    xa = jnp.concatenate(after(recv_a, spread_b[1], spread_b[4]), axis=0)
    own_a, sent_a = given(
        [dot(xa, w_gate), dot(xa, w_up)], others=spread_b[2:4], inside=packs_b
    )
    far_a = send(sent_a, flip_chip)

    recv_b = exchange(after(packs_b, sent_a))
    both_b = jnp.concatenate(after(recv_b, far_a), axis=0)
    xb, gb = both_b[:, :quarter], both_b[:, quarter:]
    own_b, sent_b = given([dot(xb, w_gate), dot(xb, w_up), dot_t(gb, w_down)])
    far_b = send(sent_b, flip_chip)

    gate_a, up_a = halves(own_a, after(far_a, sent_b))
    (hidden_a,) = whole([(jax.nn.silu(gate_a) * up_a).astype(bf16)])
    out_a = dot(hidden_a, w_down).astype(bf16)
    partial_a = combine(exchange(chunks(out_a), back=True), slot, gate, 0)

    total_a = gather_back(partial_a)
    gate_b, up_b, dh = halves(own_b, after(far_b, total_a))
    act = jax.nn.silu(gate_b)
    hidden_b, d_gate, d_up = whole(
        [
            (act * up_b).astype(bf16),
            (dh * up_b * silu_slope(gate_b)).astype(bf16),
            (dh * act).astype(bf16),
        ]
    )
    dxb = (dot_t(d_gate, w_gate) + dot_t(d_up, w_up)).astype(bf16)
    back_b = exchange(chunks(dxb), back=True)
    mixed_a = finish(after(total_a, dxb), rows)
    grad_tokens_b = finish(gather_back(combine(back_b, slot, gate, 4)), rows)
    grad_gate = t_dot(xb, d_gate).astype(bf16)
    grad_up = t_dot(xb, d_up).astype(bf16)
    grad_down = t_dot(hidden_b, gb).astype(bf16)
    return (mixed_a, grad_tokens_b, grad_gate[None], grad_up[None], grad_down[None])


def solution(mesh):
    return jax.shard_map(
        per_device,
        mesh=mesh,
        in_specs=(
            P("expert", "pipe"),
            P("expert", None),
            P("expert", None),
            P("expert", "pipe"),
            P("expert", None),
            P("expert", None),
            P("expert", "pipe"),
            P("expert", "pipe", None),
            P("expert", "pipe", None),
            P("expert", None, "pipe"),
        ),
        out_specs=(
            P("expert", "pipe"),
            P("expert", "pipe"),
            P("expert", "pipe", None),
            P("expert", "pipe", None),
            P("expert", None, "pipe"),
        ),
        check_vma=False,
    )
```
